512 devices in a mesh: var: 128 (over z, y, core), dp: 4 (over x).
Axes of the slice: x: 4, y: 8, z: 8, core: 2. Of those that a mesh axis runs over, the one named last changes fastest.
Arguments:
- fields: bfloat16 [4, 128, 256, 16], P('dp', 'var')
- presence: int32 [4, 128], P('dp'), may hold values from 0 to 1, as said below
- slot_var: int32 [128], replicated, may hold values from 0 to 127, each once
- patch_weight: bfloat16 [128, 16, 1024], P('var'), may hold values from -1.5 to 1.5
- var_embed: bfloat16 [128, 1024], P('var'), may hold values from -3 to 3
- query: float32 [1024], replicated
- key_weight: bfloat16 [1024, 1024], replicated, may hold values from -0.1875 to 0.1875
- value_weight: bfloat16 [1024, 1024], replicated, may hold values from -0.1875 to 0.1875
- out_grad: bfloat16 [4, 256, 1024], P('dp', 'var'), may hold values from -6 to 6
Outputs:
- mixed: bfloat16 [4, 256, 1024], P('dp', 'var')
- grad_patch_weight: float32 [128, 16, 1024], P('var')
- grad_var_embed: float32 [128, 1024], P('var')
- grad_query: float32 [1024], replicated
The draws below stay inside these ranges and needn't reach their ends.
Inputs may be any that keep to these rules, and one draw needn't show every extreme that they name: `presence`: every sample has at least one present variable.
All inputs are finite; a program needn't handle non-finite values.
Results may differ from the reference program's by a relative error of at most 0.0065.
The reference program's roundings to bfloat16 on the way (of `normed`, `tokens`, `key_grad`, `value_grad` and `token_grad`) count: a program that leaves them out, or rounds other values in their place, can miss the bound.
Values may be sent and summed in bfloat16 or wider, within the bound.
No kernel may reach another device: no remote copies, remote signals or barrier semaphores. Data moves between devices by JAX's collectives and lax.ppermute only.
A program may use at most 64 MiB of HBM per device.

```python
import math
import jax
import jax.numpy as jnp
from jax import lax

D = 1024
HEADS = 16
PATCH = 16
VARS = 128
PATCHES = 256
SAMPLES = 4


def draw_fields(key, part):
    key = jax.random.fold_in(key, 11)
    key_list = jax.random.split(key, 4)
    full_dims = (SAMPLES, VARS, PATCHES, PATCH)
    offset = jax.random.uniform(key_list[0], (VARS,), jnp.float32, -2.0, 2.0)
    roughness = jnp.exp(jax.random.uniform(key_list[1], (VARS,), jnp.float32, -0.7, 0.7))
    cell_scale = jnp.exp(jax.random.uniform(key_list[2], (SAMPLES, VARS, PATCHES, 1), jnp.float32, -0.7, 0.7))
    position = jnp.arange(SAMPLES, dtype=jnp.float32) / max(SAMPLES - 1, 1)
    noise_field = jnp.clip(jax.random.normal(key_list[3], full_dims, jnp.float32), -4.0, 4.0)
    sample_ramp = 1.0 + 2.0 * position
    result = offset[None, :, None, None] + sample_ramp[:, None, None, None] * roughness[None, :, None, None] * cell_scale * noise_field
    return result.astype(jnp.bfloat16)


def draw_query(key, part):
    key = jax.random.fold_in(key, 12)
    first_key, second_key = jax.random.split(key)
    low_log, high_log = (-0.7, 1.4)
    head_scale = jnp.exp(jax.random.uniform(first_key, (HEADS, 1), jnp.float32, low_log, high_log))
    entries = jnp.clip(jax.random.normal(second_key, (HEADS, D // HEADS), jnp.float32), -4.0, 4.0)
    return (head_scale * entries).reshape(D).astype(jnp.float32)


def draw_presence(key, part):
    key = jax.random.fold_in(key, 13)
    first_key, second_key = jax.random.split(key)
    coin_flips = jax.random.randint(first_key, (SAMPLES, VARS), 0, 2)
    forced = jax.random.randint(second_key, (SAMPLES, 1), 0, VARS)
    chosen = (jnp.arange(VARS, dtype=jnp.int32)[None, :] == forced).astype(jnp.int32)
    return jnp.maximum(coin_flips, chosen).astype(jnp.int32)


def steps_of(rng, shape, pieces, least, top_value):
    factor_of = 1.0
    for axis_at, blocks in pieces:
        draws = jax.random.uniform(jax.random.fold_in(jax.random.fold_in(rng, 6), axis_at), (blocks,), jnp.float32, least / len(pieces), top_value / len(pieces))
        factor_of = factor_of * jnp.repeat(jnp.exp(draws), shape[axis_at] // blocks).reshape((-1,) + (1,) * (len(shape) - 1 - axis_at))
    return factor_of


def noise(stream_key, dims, scale, limit, cuts=(), kind=jnp.bfloat16):
    values = jax.random.normal(stream_key, dims, jnp.float32) * scale
    if len(cuts) > 0:
        values = steps_of(stream_key, dims, cuts, -0.22, 0.18) * values
    return jnp.clip(values, min=-limit, max=limit).astype(kind)


def setup_inputs(seed: int = 0) -> dict:
    keys = jax.random.split(jax.random.key(seed), 10)
    fields = draw_fields(jax.random.fold_in(keys[9], 71), 0)
    presence = draw_presence(jax.random.fold_in(keys[9], 71), 0)
    slot_var = jax.random.permutation(keys[2], VARS).astype(jnp.int32)
    patch_weight = noise(keys[3], (VARS, PATCH, D), PATCH ** -0.5, 1.5, ((0, 128),))
    var_embed = noise(keys[4], (VARS, D), 0.5, 3.0, ((0, 128),))
    query = draw_query(jax.random.fold_in(keys[9], 71), 0)
    key_weight = noise(keys[6], (D, D), D ** -0.5, 0.1875)
    value_weight = noise(keys[7], (D, D), D ** -0.5, 0.1875)
    out_grad = noise(keys[8], (SAMPLES, PATCHES, D), 1.0, 6.0, ((0, 4), (1, 128)))
    return {"fields": fields, "presence": presence, "slot_var": slot_var, "patch_weight": patch_weight, "var_embed": var_embed, "query": query, "key_weight": key_weight, "value_weight": value_weight, "out_grad": out_grad}


field_eps = 1e-05
key_eps = 1e-06
masked_low = -1e+30
highest = lax.Precision.HIGHEST

def slot_presence(presence, slot_var):
    lookup = (slot_var[:, None] == jnp.arange(presence.shape[1], dtype=jnp.int32)[None, :]).astype(jnp.int32)
    return lax.optimization_barrier(jnp.sum(presence[:, None, :] * lookup[None, :, :], axis=2))

def masked_softmax(scores, valid_mask):
    row_max = lax.optimization_barrier(jnp.max(jnp.where(valid_mask, scores, masked_low), axis=-1, keepdims=True))
    weights = jnp.where(valid_mask, jnp.exp(scores - row_max), 0.0)
    return weights / lax.optimization_barrier(jnp.sum(weights, axis=-1, keepdims=True))

def as_bf16(source):
    return lax.optimization_barrier(source.astype(jnp.bfloat16)).astype(jnp.float32)

def reference(fields, presence, slot_var, patch_weight, var_embed, query, key_weight, value_weight, out_grad):
    head_dim = D // HEADS
    score_scale = 1.0 / math.sqrt(head_dim)
    flag_rows = slot_presence(presence, slot_var).astype(jnp.float32)
    values = fields.astype(jnp.float32)
    cell_total = jnp.maximum(lax.optimization_barrier(jnp.sum(flag_rows, axis=0)), 1.0) * (PATCHES * PATCH)
    mean_value = lax.optimization_barrier(jnp.sum(flag_rows[:, :, None, None] * values, axis=(0, 2, 3))) / cell_total
    centered = values - mean_value[None, :, None, None]
    spread = lax.optimization_barrier(jnp.sum(flag_rows[:, :, None, None] * centered * centered, axis=(0, 2, 3))) / cell_total
    normed = (centered * lax.rsqrt(spread + field_eps)[None, :, None, None]).astype(jnp.bfloat16)
    block_size = math.gcd(PATCHES, 64)
    blocks = PATCHES // block_size
    normed_blocks = normed.reshape(SAMPLES, VARS, blocks, block_size, PATCH).transpose(0, 2, 1, 3, 4)
    normed_blocks = normed_blocks.reshape(SAMPLES * blocks, VARS, block_size, PATCH)
    grad_blocks = out_grad.reshape(SAMPLES * blocks, block_size, D)
    flag_blocks = jnp.repeat(flag_rows, blocks, axis=0)
    weight_f = patch_weight.astype(jnp.float32)
    embed_f = var_embed.astype(jnp.float32)
    key_f = key_weight.astype(jnp.float32)
    value_f = value_weight.astype(jnp.float32)
    value_heads = value_f.reshape(D, HEADS, head_dim)
    query_heads = query.reshape(HEADS, head_dim)

    def block_step(running, inputs):
        normed_blk, grad_blk, flag_line = inputs
        normed_f = normed_blk.astype(jnp.float32)
        tokens = jnp.einsum('spe,sed->spd', normed_f, weight_f, precision=highest) + embed_f[:, None, :]
        tokens_f = as_bf16(tokens)
        raw_keys = jnp.dot(tokens_f.reshape(-1, D), key_f, preferred_element_type=jnp.float32)
        raw_keys = raw_keys.reshape(VARS, block_size, HEADS, head_dim)
        key_ratio = lax.rsqrt(lax.optimization_barrier(jnp.mean(raw_keys * raw_keys, axis=-1)) + key_eps)
        normed_keys = raw_keys * key_ratio[..., None]
        scores = jnp.einsum('sphe,he->phs', normed_keys, query_heads, precision=highest) * score_scale
        attention = masked_softmax(scores, flag_line[None, None, :] > 0)
        summed = jnp.einsum('phs,spd->phd', attention, tokens_f, precision=highest)
        heads_out = jnp.einsum('phd,dhe->phe', summed, value_heads, precision=highest)
        mixed_out = heads_out.reshape(block_size, D).astype(jnp.bfloat16)
        grad_f = grad_blk.astype(jnp.float32).reshape(block_size, HEADS, head_dim)
        lifted = jnp.einsum('phe,dhe->phd', grad_f, value_heads, precision=highest)
        attn_grad = jnp.einsum('phd,spd->phs', lifted, tokens_f, precision=highest)
        dscore = attention * (attn_grad - lax.optimization_barrier(jnp.sum(attention * attn_grad, axis=-1, keepdims=True)))
        dscore_t = jnp.transpose(dscore, (2, 0, 1))
        attention_t = jnp.transpose(attention, (2, 0, 1))
        norm_grad = dscore_t[..., None] * query_heads * score_scale
        key_grad = key_ratio[..., None] * (norm_grad - normed_keys * lax.optimization_barrier(jnp.mean(norm_grad * normed_keys, axis=-1, keepdims=True)))
        value_grad = attention_t[..., None] * grad_f[None]
        key_grad_b = as_bf16(key_grad).reshape(-1, D)
        value_grad_b = as_bf16(value_grad).reshape(-1, D)
        token_grad = jnp.dot(key_grad_b, key_f.T, preferred_element_type=jnp.float32)
        token_grad = token_grad + jnp.dot(value_grad_b, value_f.T, preferred_element_type=jnp.float32)
        token_grad = as_bf16(token_grad).reshape(VARS, block_size, D)
        dweight = jnp.einsum('spe,spd->sed', normed_f, token_grad, precision=highest)
        dembed = lax.optimization_barrier(jnp.sum(token_grad, axis=1))
        dquery = jnp.einsum('phs,sphe->he', dscore, normed_keys, precision=highest) * score_scale
        running = (running[0] + dweight, running[1] + dembed, running[2] + dquery)
        return (running, mixed_out)
    start = (jnp.zeros((VARS, PATCH, D), jnp.float32), jnp.zeros((VARS, D), jnp.float32), jnp.zeros((HEADS, head_dim), jnp.float32))
    running, mixed_all = lax.scan(block_step, start, (normed_blocks, grad_blocks, flag_blocks))
    mixed = mixed_all.reshape(SAMPLES, PATCHES, D)
    return (mixed, running[0], running[1], running[2].reshape(D))
```

```python
import math

import jax
import jax.numpy as jnp
from jax import lax
from jax.experimental import pallas as pl
from jax.experimental.pallas import tpu as pltpu
from jax.sharding import PartitionSpec as P

HEADS = 16
LANES = 128
SPAN = 256

field_eps = 1e-05
key_eps = 1e-06
masked_low = -1e30

f32 = jnp.float32
bf16 = jnp.bfloat16


def params(mib):
    return pltpu.CompilerParams(vmem_limit_bytes=mib * 2**20)


def stats_kernel(presence_ref, slot_ref, fields_ref, out_ref):
    own = lax.axis_index("var")
    flag = presence_ref[0, slot_ref[own]].astype(f32)
    values = fields_ref[...].astype(f32)
    cells = values.shape[0] * values.shape[1]
    total = jnp.sum(jnp.sum(values, axis=0, keepdims=True), axis=1, keepdims=True)
    centered = values - total / cells
    squares = jnp.sum(jnp.sum(centered * centered, axis=0, keepdims=True), axis=1, keepdims=True)
    row = lax.broadcasted_iota(jnp.int32, out_ref.shape, 0)
    out_ref[...] = jnp.where(row == 0, total, jnp.where(row == 1, squares, 1.0)) * flag


def token_kernel(stats_ref, fields_ref, weight_ref, embed_ref, tokens_ref, normed_ref, rows, parts):
    patches, pixels = fields_ref.shape
    cells = float(patches * pixels)
    groups = weight_ref.shape[1] // LANES
    samples = stats_ref.shape[0]
    sums = [stats_ref[b, 0:1, :] for b in range(samples)]
    flags = [stats_ref[b, 2:3, :] for b in range(samples)]
    cell_total = jnp.maximum(sum(flags[1:], flags[0]), 1.0) * cells
    mean = sum(sums[1:], sums[0]) / cell_total
    second = jnp.zeros_like(mean)
    for b in range(samples):
        shift = sums[b] / cells - mean
        second = second + stats_ref[b, 1:2, :] + flags[b] * cells * shift * shift
    scale = lax.rsqrt(second / cell_total + field_eps)
    normed = ((fields_ref[...].astype(f32) - mean[:, :pixels]) * scale[:, :pixels]).astype(bf16)
    tokens = jnp.dot(normed, weight_ref[...], preferred_element_type=f32)
    tokens = tokens + embed_ref[...].astype(f32)
    for j in range(groups):
        rows[pl.ds(j, patches, stride=groups), :] = tokens[:, j * LANES : (j + 1) * LANES]
    tokens_ref[...] = rows[...].reshape(tokens_ref.shape).astype(bf16)
    lane = lax.broadcasted_iota(jnp.int32, parts.shape, 1)
    parts[...] = jnp.where(lane == pixels, 1.0, 0.0)
    parts[:, :pixels] = normed.astype(f32)
    half = patches // 2
    for p in range(2):
        normed_ref[p * half : (p + 1) * half, :] = parts[pl.ds(p, half, stride=2), :].astype(bf16)


def head_rows(width):
    row = lax.broadcasted_iota(jnp.int32, (width, LANES), 0)
    lane = lax.broadcasted_iota(jnp.int32, (width, LANES), 1)
    head = row // (width // HEADS)
    return jnp.where((lane % HEADS == head) & (lane < 3 * HEADS), 1.0, 0.0).astype(bf16)


def head_lanes(width):
    row = lax.broadcasted_iota(jnp.int32, (LANES, width), 0)
    lane = lax.broadcasted_iota(jnp.int32, (LANES, width), 1)
    head = lane // (width // HEADS)
    return jnp.where((row % HEADS == head) & (row < 3 * HEADS), 1.0, 0.0).astype(bf16)


def head_sums(values, selector):
    high = values.astype(bf16)
    low = (values - high.astype(f32)).astype(bf16)
    return jnp.dot(high, selector, preferred_element_type=f32) + jnp.dot(
        low, selector, preferred_element_type=f32
    )


def three_parts(values):
    lane = lax.broadcasted_iota(jnp.int32, values.shape, 1)
    high = values.astype(bf16).astype(f32)
    rest = values - high
    middle = rest.astype(bf16).astype(f32)
    low = rest - middle
    parts = jnp.where(lane < HEADS, high, jnp.where(lane < 2 * HEADS, middle, low))
    return parts.astype(bf16)


def mix_kernel(
    presence_ref,
    slot_ref,
    recv_ref,
    key_ref,
    value_ref,
    query_ref,
    grad_ref,
    mixed_ref,
    send_ref,
    arrived,
    tokens,
    keys,
    values,
    key_grad,
    value_grad,
    leaving,
):
    slots, recv_rows, _ = recv_ref.shape
    width = key_ref.shape[0]
    groups = width // LANES
    send_rows = send_ref.shape[1]
    head_dim = width // HEADS
    score_scale = 1.0 / math.sqrt(head_dim)
    pairs = recv_rows // groups
    spans = [slice(c, c + SPAN) for c in range(0, width, SPAN)]
    halves = [slice(p * slots, (p + 1) * slots) for p in range(pairs)]

    arrived[...] = recv_ref[...].astype(f32).reshape(arrived.shape)
    for p in range(pairs):
        for j in range(groups):
            block = arrived[pl.ds(p * groups + j, slots, stride=recv_rows), :]
            tokens[halves[p], j * LANES : (j + 1) * LANES] = block.astype(bf16)

    row = lax.broadcasted_iota(jnp.int32, (LANES, slots), 0)
    lookup = jnp.where(row == slot_ref[...], 1.0, 0.0).astype(bf16)
    present = jnp.broadcast_to(presence_ref[...].astype(f32), (slots, LANES)).astype(bf16)
    present = jnp.dot(present, lookup, preferred_element_type=f32)
    valid = jnp.transpose(present) > 0.5

    query = query_ref[...]
    grad = grad_ref[...].astype(f32)
    selector = head_rows(width)
    spread = head_lanes(width)

    squares = jnp.zeros((pairs * slots, LANES), f32)
    raw = jnp.zeros((pairs * slots, LANES), f32)
    attn_grad = jnp.zeros((pairs * slots, LANES), f32)
    for span in spans:
        block = jnp.dot(tokens[...], key_ref[:, span], preferred_element_type=f32)
        keys[:, span] = block
        squares = squares + head_sums(block * block, selector[span])
        raw = raw + head_sums(block * query[:, span], selector[span])
    for span in spans:
        block = jnp.dot(tokens[...], value_ref[:, span], preferred_element_type=f32)
        values[:, span] = block
        product = jnp.concatenate([block[halves[p]] * grad[p : p + 1, span] for p in range(pairs)], axis=0)
        attn_grad = attn_grad + head_sums(product, selector[span])

    ratio = lax.rsqrt(squares * (1.0 / head_dim) + key_eps)
    scores = raw * ratio * score_scale
    attention, dscore = [], []
    for p in range(pairs):
        part = scores[halves[p]]
        top = jnp.max(jnp.where(valid, part, masked_low), axis=0, keepdims=True)
        weights = jnp.where(valid, jnp.exp(part - top), 0.0)
        weights = weights / jnp.sum(weights, axis=0, keepdims=True)
        change = attn_grad[halves[p]]
        inner = jnp.sum(weights * change, axis=0, keepdims=True)
        attention.append(weights)
        dscore.append(weights * (change - inner))
    attention = jnp.concatenate(attention, axis=0)
    dscore = jnp.concatenate(dscore, axis=0)
    along = dscore * ratio * score_scale
    across = dscore * scores * ratio * ratio * (1.0 / head_dim)
    attention_parts = three_parts(attention)
    along_parts = three_parts(along)
    across_parts = three_parts(across)

    for span in spans:
        weights = jnp.dot(attention_parts, spread[:, span], preferred_element_type=f32)
        first = jnp.dot(along_parts, spread[:, span], preferred_element_type=f32)
        second = jnp.dot(across_parts, spread[:, span], preferred_element_type=f32)
        key_block = keys[:, span]
        key_grad[:, span] = (first * query[:, span] - second * key_block).astype(bf16)
        dquery = jnp.sum(first * key_block, axis=0, keepdims=True)
        for p in range(pairs):
            part = weights[halves[p]]
            value_grad[halves[p], span] = (part * grad[p : p + 1, span]).astype(bf16)
            mixed_ref[p : p + 1, span] = jnp.sum(
                part * values[halves[p], span], axis=0, keepdims=True
            ).astype(bf16)
        for i in range(SPAN // LANES):
            j = span.start // LANES + i
            line = dquery[:, i * LANES : (i + 1) * LANES]
            leaving[pl.ds(pairs * groups + j, slots, stride=send_rows), :] = jnp.broadcast_to(
                line, (slots, LANES)
            )

    contract = (((1,), (1,)), ((), ()))
    for span in spans:
        block = lax.dot_general(key_grad[...], key_ref[span, :], contract, preferred_element_type=f32)
        block = block + lax.dot_general(
            value_grad[...], value_ref[span, :], contract, preferred_element_type=f32
        )
        for p in range(pairs):
            for i in range(SPAN // LANES):
                j = span.start // LANES + i
                leaving[pl.ds(p * groups + j, slots, stride=send_rows), :] = block[
                    halves[p], i * LANES : (i + 1) * LANES
                ]
    send_ref[...] = leaving[...].reshape(send_ref.shape).astype(bf16)


def grad_kernel(recv_ref, normed_ref, out_ref, arrived, grads):
    owners, recv_rows, _ = recv_ref.shape
    width = grads.shape[1]
    groups = width // LANES
    pairs = recv_rows // groups - 1
    pixels = out_ref.shape[0] // groups - 2
    blocks = recv_ref[...].astype(f32)
    arrived[...] = blocks.reshape(arrived.shape)
    dquery = jnp.sum(blocks[:, pairs * groups :, :], axis=0)
    for p in range(pairs):
        for j in range(groups):
            block = arrived[pl.ds(p * groups + j, owners, stride=recv_rows), :]
            grads[p * owners : (p + 1) * owners, j * LANES : (j + 1) * LANES] = block.astype(bf16)
    sums = lax.dot_general(
        normed_ref[...], grads[...], (((0,), (0,)), ((), ())), preferred_element_type=f32
    )
    for j in range(groups):
        lanes = slice(j * LANES, (j + 1) * LANES)
        out_ref[j * pixels : (j + 1) * pixels, :] = sums[:pixels, lanes]
        out_ref[groups * pixels + j : groups * pixels + j + 1, :] = sums[pixels : pixels + 1, lanes]
    out_ref[groups * (pixels + 1) :, :] = dquery


def total_kernel(parts_ref, weight_ref, embed_ref, query_ref):
    pixels, width = weight_ref.shape
    groups = width // LANES
    total = (parts_ref[0] + parts_ref[1]) + (parts_ref[2] + parts_ref[3])
    for j in range(groups):
        lanes = slice(j * LANES, (j + 1) * LANES)
        weight_ref[:, lanes] = total[j * pixels : (j + 1) * pixels]
        embed_ref[:, lanes] = total[groups * pixels + j : groups * pixels + j + 1]
        query_ref[:, lanes] = total[groups * (pixels + 1) + j : groups * (pixels + 1) + j + 1]


smem = pl.BlockSpec(memory_space=pltpu.SMEM)
vmem = pl.BlockSpec(memory_space=pltpu.VMEM)


def on_device(
    fields, presence, slot_var, patch_weight, var_embed, query, key_weight, value_weight, out_grad
):
    var_count = lax.axis_size("var")
    _, _, patches, pixels = fields.shape
    width = key_weight.shape[0]
    groups = width // LANES
    slots = slot_var.shape[0]
    pairs = patches // var_count
    rows = pairs * groups
    fields = fields.reshape(patches, pixels)

    stats = pl.pallas_call(
        stats_kernel,
        out_shape=jax.ShapeDtypeStruct((8, LANES), f32),
        in_specs=[smem, smem, vmem],
        out_specs=vmem,
        name="stats",
    )(presence, slot_var, fields)
    stats = lax.all_gather(stats, "dp")

    tokens, normed = pl.pallas_call(
        token_kernel,
        out_shape=(
            jax.ShapeDtypeStruct((var_count, rows, LANES), bf16),
            jax.ShapeDtypeStruct((patches, LANES), bf16),
        ),
        in_specs=[vmem] * 4,
        out_specs=(vmem, vmem),
        scratch_shapes=[pltpu.VMEM((patches * groups, LANES), f32), pltpu.VMEM((patches, LANES), f32)],
        compiler_params=params(16),
        name="tokens",
    )(stats, fields, patch_weight.reshape(pixels, width), var_embed)
    gathered = lax.all_to_all(tokens, "var", split_axis=0, concat_axis=0, tiled=True)

    mixed, outgoing = pl.pallas_call(
        mix_kernel,
        out_shape=(
            jax.ShapeDtypeStruct((pairs, width), bf16),
            jax.ShapeDtypeStruct((slots, rows + groups, LANES), bf16),
        ),
        in_specs=[vmem] * 7,
        out_specs=(vmem, vmem),
        scratch_shapes=[
            pltpu.VMEM((slots * rows, LANES), f32),
            pltpu.VMEM((pairs * slots, width), bf16),
            pltpu.VMEM((pairs * slots, width), f32),
            pltpu.VMEM((pairs * slots, width), f32),
            pltpu.VMEM((pairs * slots, width), bf16),
            pltpu.VMEM((pairs * slots, width), bf16),
            pltpu.VMEM((slots * (rows + groups), LANES), f32),
        ],
        compiler_params=params(32),
        name="mix",
    )(
        presence,
        slot_var.reshape(1, slots),
        gathered,
        key_weight,
        value_weight,
        query.reshape(1, width),
        out_grad.reshape(pairs, width),
    )
    returned = lax.all_to_all(outgoing, "var", split_axis=0, concat_axis=0, tiled=True)

    parts = pl.pallas_call(
        grad_kernel,
        out_shape=jax.ShapeDtypeStruct((groups * (pixels + 2), LANES), f32),
        in_specs=[vmem, vmem],
        out_specs=vmem,
        scratch_shapes=[
            pltpu.VMEM((var_count * (rows + groups), LANES), f32),
            pltpu.VMEM((patches, width), bf16),
        ],
        compiler_params=params(16),
        name="grads",
    )(returned, normed)
    parts = lax.all_gather(parts, "dp")

    dweight, dembed, dquery = pl.pallas_call(
        total_kernel,
        out_shape=(
            jax.ShapeDtypeStruct((pixels, width), f32),
            jax.ShapeDtypeStruct((1, width), f32),
            jax.ShapeDtypeStruct((1, width), f32),
        ),
        in_specs=[vmem],
        out_specs=(vmem, vmem, vmem),
        name="totals",
    )(parts)
    return (
        mixed.reshape(1, pairs, width),
        dweight.reshape(1, pixels, width),
        dembed,
        dquery.reshape(width),
    )


def solution(mesh):
    return jax.shard_map(
        on_device,
        mesh=mesh,
        in_specs=(
            P("dp", "var", None, None),
            P("dp", None),
            P(),
            P("var", None, None),
            P("var", None),
            P(),
            P(),
            P(),
            P("dp", "var", None),
        ),
        out_specs=(P("dp", "var", None), P("var", None, None), P("var", None), P()),
        check_vma=False,
    )
```

```python
import math

import jax
import jax.numpy as jnp
from jax import lax
from jax.experimental import pallas as pl
from jax.experimental.pallas import tpu as pltpu
from jax.sharding import PartitionSpec as P

HEADS = 16
LANES = 128
SPAN = 256
FLOPS, BYTES = 6_000_000_000, 2_000_000

field_eps = 1e-05
key_eps = 1e-06
masked_low = -1e30

f32 = jnp.float32
bf16 = jnp.bfloat16


def params(mib):
    return pltpu.CompilerParams(vmem_limit_bytes=mib * 2**20)


def stats_kernel(
    presence_ref,
    slot_ref,
    fields_ref,
    weight_ref,
    embed_ref,
    presence_row,
    slot_row,
    query_ref,
    grad_ref,
    stats_ref,
    fields_out,
    weight_out,
    embed_out,
    presence_out,
    slot_out,
    query_out,
    grad_out,
    arrivals,
):
    moves = [
        pltpu.make_async_copy(source, target, arrivals.at[i])
        for i, (source, target) in enumerate(
            (
                (fields_ref, fields_out),
                (weight_ref, weight_out),
                (embed_ref, embed_out),
                (presence_row, presence_out),
                (slot_row, slot_out),
                (query_ref, query_out),
                (grad_ref, grad_out),
            )
        )
    ]
    for move in moves:
        move.start()
    own = lax.axis_index("var")
    flag = presence_ref[0, slot_ref[own]].astype(f32)
    moves[0].wait()
    values = fields_out[...].astype(f32)
    cells = values.shape[0] * values.shape[1]
    total = jnp.sum(jnp.sum(values, axis=0, keepdims=True), axis=1, keepdims=True)
    centered = values - total / cells
    squares = jnp.sum(jnp.sum(centered * centered, axis=0, keepdims=True), axis=1, keepdims=True)
    lane = lax.broadcasted_iota(jnp.int32, stats_ref.shape, 1)
    stats_ref[...] = jnp.where(lane == 0, total, jnp.where(lane == 1, squares, 1.0)) * flag
    for move in moves[1:]:
        move.wait()


def token_kernel(stats_ref, fields_ref, weight_ref, embed_ref, tokens_ref, normed_ref, rows, parts):
    pixels, patches = fields_ref.shape
    cells = float(patches * pixels)
    groups = weight_ref.shape[1] // LANES
    samples = stats_ref.shape[0]
    sums = [stats_ref[b, :, 0:1] for b in range(samples)]
    flags = [stats_ref[b, :, 2:3] for b in range(samples)]
    cell_total = jnp.maximum(sum(flags[1:], flags[0]), 1.0) * cells
    mean = sum(sums[1:], sums[0]) / cell_total
    second = jnp.zeros_like(mean)
    for b in range(samples):
        shift = sums[b] / cells - mean
        second = second + stats_ref[b, :, 1:2] + flags[b] * cells * shift * shift
    scale = lax.rsqrt(second / cell_total + field_eps)
    row = lax.broadcasted_iota(jnp.int32, (LANES, patches), 0)
    upright = jnp.concatenate(
        [(fields_ref[...].astype(f32) - mean) * scale, jnp.zeros((LANES - pixels, patches), f32)], axis=0
    )
    normed = jnp.transpose(jnp.where(row == pixels, 1.0, upright))
    parts[...] = normed.astype(bf16).astype(f32)
    tokens = jnp.dot(normed[:, :pixels].astype(bf16), weight_ref[...], preferred_element_type=f32)
    tokens = tokens + embed_ref[...].astype(f32)
    for j in range(groups):
        rows[pl.ds(j, patches, stride=groups), :] = tokens[:, j * LANES : (j + 1) * LANES]
    tokens_ref[...] = rows[...].reshape(tokens_ref.shape).astype(bf16)
    half = patches // 2
    for p in range(2):
        normed_ref[p * half : (p + 1) * half, :] = parts[pl.ds(p, half, stride=2), :].astype(bf16)


def head_rows(width):
    row = lax.broadcasted_iota(jnp.int32, (width, LANES), 0)
    lane = lax.broadcasted_iota(jnp.int32, (width, LANES), 1)
    head = row // (width // HEADS)
    return jnp.where((lane % HEADS == head) & (lane < 3 * HEADS), 1.0, 0.0).astype(bf16)


def head_lanes(width):
    row = lax.broadcasted_iota(jnp.int32, (LANES, width), 0)
    lane = lax.broadcasted_iota(jnp.int32, (LANES, width), 1)
    head = lane // (width // HEADS)
    return jnp.where((row % HEADS == head) & (row < 3 * HEADS), 1.0, 0.0).astype(bf16)


def head_sums(values, selector):
    high = values.astype(bf16)
    low = (values - high.astype(f32)).astype(bf16)
    return jnp.dot(high, selector, preferred_element_type=f32) + jnp.dot(
        low, selector, preferred_element_type=f32
    )


def three_parts(values):
    lane = lax.broadcasted_iota(jnp.int32, values.shape, 1)
    high = values.astype(bf16).astype(f32)
    rest = values - high
    middle = rest.astype(bf16).astype(f32)
    low = rest - middle
    parts = jnp.where(lane < HEADS, high, jnp.where(lane < 2 * HEADS, middle, low))
    return parts.astype(bf16)


def mix_kernel(
    presence_ref,
    slot_ref,
    recv_ref,
    key_ref,
    value_ref,
    query_ref,
    grad_ref,
    mixed_ref,
    send_ref,
    arrived,
    tokens,
    keys,
    values,
    key_grad,
    value_grad,
    leaving,
):
    slots, recv_rows, _ = recv_ref.shape
    width = key_ref.shape[0]
    groups = width // LANES
    send_rows = send_ref.shape[1]
    head_dim = width // HEADS
    score_scale = 1.0 / math.sqrt(head_dim)
    pairs = recv_rows // groups
    spans = [slice(c, c + SPAN) for c in range(0, width, SPAN)]
    halves = [slice(p * slots, (p + 1) * slots) for p in range(pairs)]

    arrived[...] = recv_ref[...].astype(f32).reshape(arrived.shape)
    for p in range(pairs):
        for j in range(groups):
            block = arrived[pl.ds(p * groups + j, slots, stride=recv_rows), :]
            tokens[halves[p], j * LANES : (j + 1) * LANES] = block.astype(bf16)

    row = lax.broadcasted_iota(jnp.int32, (LANES, slots), 0)
    lookup = jnp.where(row == slot_ref[...], 1.0, 0.0).astype(bf16)
    present = jnp.broadcast_to(presence_ref[...].astype(f32), (slots, LANES)).astype(bf16)
    present = jnp.dot(present, lookup, preferred_element_type=f32)
    valid = jnp.transpose(present) > 0.5

    query = query_ref[...]
    grad = grad_ref[...].astype(f32)
    selector = head_rows(width)
    spread = head_lanes(width)

    squares = jnp.zeros((pairs * slots, LANES), f32)
    raw = jnp.zeros((pairs * slots, LANES), f32)
    attn_grad = jnp.zeros((pairs * slots, LANES), f32)
    for span in spans:
        block = jnp.dot(tokens[...], key_ref[:, span], preferred_element_type=f32)
        keys[:, span] = block
        squares = squares + head_sums(block * block, selector[span])
        raw = raw + head_sums(block * query[:, span], selector[span])
    for span in spans:
        block = jnp.dot(tokens[...], value_ref[:, span], preferred_element_type=f32)
        values[:, span] = block
        product = jnp.concatenate([block[halves[p]] * grad[p : p + 1, span] for p in range(pairs)], axis=0)
        attn_grad = attn_grad + head_sums(product, selector[span])

    ratio = lax.rsqrt(squares * (1.0 / head_dim) + key_eps)
    scores = raw * ratio * score_scale
    attention, dscore = [], []
    for p in range(pairs):
        part = scores[halves[p]]
        top = jnp.max(jnp.where(valid, part, masked_low), axis=0, keepdims=True)
        weights = jnp.where(valid, jnp.exp(part - top), 0.0)
        weights = weights / jnp.sum(weights, axis=0, keepdims=True)
        change = attn_grad[halves[p]]
        inner = jnp.sum(weights * change, axis=0, keepdims=True)
        attention.append(weights)
        dscore.append(weights * (change - inner))
    attention = jnp.concatenate(attention, axis=0)
    dscore = jnp.concatenate(dscore, axis=0)
    along = dscore * ratio * score_scale
    across = dscore * scores * ratio * ratio * (1.0 / head_dim)
    attention_parts = three_parts(attention)
    along_parts = three_parts(along)
    across_parts = three_parts(across)

    for span in spans:
        weights = jnp.dot(attention_parts, spread[:, span], preferred_element_type=f32)
        first = jnp.dot(along_parts, spread[:, span], preferred_element_type=f32)
        second = jnp.dot(across_parts, spread[:, span], preferred_element_type=f32)
        key_block = keys[:, span]
        key_grad[:, span] = (first * query[:, span] - second * key_block).astype(bf16)
        dquery = jnp.sum(first * key_block, axis=0, keepdims=True)
        for p in range(pairs):
            part = weights[halves[p]]
            value_grad[halves[p], span] = (part * grad[p : p + 1, span]).astype(bf16)
            mixed_ref[p : p + 1, span] = jnp.sum(
                part * values[halves[p], span], axis=0, keepdims=True
            ).astype(bf16)
        for i in range(SPAN // LANES):
            j = span.start // LANES + i
            line = dquery[:, i * LANES : (i + 1) * LANES]
            leaving[pl.ds(pairs * groups + j, slots, stride=send_rows), :] = jnp.broadcast_to(
                line, (slots, LANES)
            )

    contract = (((1,), (1,)), ((), ()))
    for span in spans:
        block = lax.dot_general(key_grad[...], key_ref[span, :], contract, preferred_element_type=f32)
        block = block + lax.dot_general(
            value_grad[...], value_ref[span, :], contract, preferred_element_type=f32
        )
        for p in range(pairs):
            for i in range(SPAN // LANES):
                j = span.start // LANES + i
                leaving[pl.ds(p * groups + j, slots, stride=send_rows), :] = block[
                    halves[p], i * LANES : (i + 1) * LANES
                ]
    send_ref[...] = leaving[...].reshape(send_ref.shape).astype(bf16)


def grad_kernel(recv_ref, normed_ref, out_ref, arrived, grads):
    owners, recv_rows, _ = recv_ref.shape
    width = grads.shape[1]
    groups = width // LANES
    pairs = recv_rows // groups - 1
    copies, out_rows, _ = out_ref.shape
    pixels = out_rows // groups - 2
    blocks = recv_ref[...].astype(f32)
    arrived[...] = blocks.reshape(arrived.shape)
    dquery = jnp.sum(blocks[:, pairs * groups :, :], axis=0)
    for p in range(pairs):
        for j in range(groups):
            block = arrived[pl.ds(p * groups + j, owners, stride=recv_rows), :]
            grads[p * owners : (p + 1) * owners, j * LANES : (j + 1) * LANES] = block.astype(bf16)
    sums = lax.dot_general(
        normed_ref[...], grads[...], (((0,), (0,)), ((), ())), preferred_element_type=f32
    )
    for j in range(groups):
        lanes = slice(j * LANES, (j + 1) * LANES)
        for c in range(copies):
            out_ref[c, j * pixels : (j + 1) * pixels, :] = sums[:pixels, lanes]
            out_ref[c, groups * pixels + j : groups * pixels + j + 1, :] = sums[
                pixels : pixels + 1, lanes
            ]
    for c in range(copies):
        out_ref[c, groups * (pixels + 1) :, :] = dquery


def total_kernel(parts_ref, weight_ref, embed_ref, query_ref):
    pixels, width = weight_ref.shape
    groups = width // LANES
    total = (parts_ref[0] + parts_ref[1]) + (parts_ref[2] + parts_ref[3])
    for j in range(groups):
        lanes = slice(j * LANES, (j + 1) * LANES)
        weight_ref[:, lanes] = total[j * pixels : (j + 1) * pixels]
        embed_ref[:, lanes] = total[groups * pixels + j : groups * pixels + j + 1]
        query_ref[:, lanes] = total[groups * (pixels + 1) + j : groups * (pixels + 1) + j + 1]


smem = pl.BlockSpec(memory_space=pltpu.SMEM)
vmem = pl.BlockSpec(memory_space=pltpu.VMEM)
hbm = pl.BlockSpec(memory_space=pltpu.HBM)


def on_device(
    fields, presence, slot_var, patch_weight, var_embed, query, key_weight, value_weight, out_grad
):
    var_count = lax.axis_size("var")
    _, _, patches, pixels = fields.shape
    width = key_weight.shape[0]
    groups = width // LANES
    slots = slot_var.shape[0]
    pairs = patches // var_count
    rows = pairs * groups
    samples = lax.axis_size("dp")
    fixed = tuple(
        pltpu.with_memory_space_constraint(a, pltpu.HBM)
        for a in (
            jnp.transpose(fields.reshape(patches, pixels)),
        patch_weight.reshape(pixels, width),
        var_embed,
        presence,
        slot_var.reshape(1, slots),
        query.reshape(1, width),
        out_grad.reshape(pairs, width),
        )
    )

    stats, fields, patch_weight, var_embed, present, slot_row, query_row, grad_rows = pl.pallas_call(
        stats_kernel,
        out_shape=(jax.ShapeDtypeStruct((1, LANES), f32),)
        + tuple(pltpu.VMEM(a.shape, a.dtype) for a in fixed),
        in_specs=[smem, smem] + [hbm] * len(fixed),
        out_specs=[vmem] * (1 + len(fixed)),
        scratch_shapes=[pltpu.SemaphoreType.DMA((len(fixed),))],
        name="stats",
    )(presence, slot_var, *fixed)
    stats = lax.all_gather(stats, "dp")

    tokens, normed = pl.pallas_call(
        token_kernel,
        out_shape=(
            jax.ShapeDtypeStruct((var_count, rows, LANES), bf16),
            jax.ShapeDtypeStruct((patches, LANES), bf16),
        ),
        in_specs=[vmem] * 4,
        out_specs=(vmem, vmem),
        scratch_shapes=[pltpu.VMEM((patches * groups, LANES), f32), pltpu.VMEM((patches, LANES), f32)],
        compiler_params=params(16),
        cost_estimate=pl.CostEstimate(flops=FLOPS, bytes_accessed=BYTES, transcendentals=0),
        name="tokens",
    )(stats, fields, patch_weight, var_embed)
    gathered = lax.all_to_all(tokens, "var", split_axis=0, concat_axis=0, tiled=True)

    mixed, outgoing = pl.pallas_call(
        mix_kernel,
        out_shape=(
            jax.ShapeDtypeStruct((pairs, width), bf16),
            jax.ShapeDtypeStruct((slots, rows + groups, LANES), bf16),
        ),
        in_specs=[vmem] * 7,
        out_specs=(vmem, vmem),
        scratch_shapes=[
            pltpu.VMEM((slots * rows, LANES), f32),
            pltpu.VMEM((pairs * slots, width), bf16),
            pltpu.VMEM((pairs * slots, width), f32),
            pltpu.VMEM((pairs * slots, width), f32),
            pltpu.VMEM((pairs * slots, width), bf16),
            pltpu.VMEM((pairs * slots, width), bf16),
            pltpu.VMEM((slots * (rows + groups), LANES), f32),
        ],
        compiler_params=params(32),
        name="mix",
    )(present, slot_row, gathered, key_weight, value_weight, query_row, grad_rows)
    returned = lax.all_to_all(outgoing, "var", split_axis=0, concat_axis=0, tiled=True)

    parts = pl.pallas_call(
        grad_kernel,
        out_shape=jax.ShapeDtypeStruct((samples, groups * (pixels + 2), LANES), f32),
        in_specs=[vmem, vmem],
        out_specs=vmem,
        scratch_shapes=[
            pltpu.VMEM((var_count * (rows + groups), LANES), f32),
            pltpu.VMEM((patches, width), bf16),
        ],
        compiler_params=params(16),
        name="grads",
    )(returned, normed)
    parts = lax.all_to_all(parts, "dp", split_axis=0, concat_axis=0, tiled=True)

    dweight, dembed, dquery = pl.pallas_call(
        total_kernel,
        out_shape=(
            jax.ShapeDtypeStruct((pixels, width), f32),
            jax.ShapeDtypeStruct((1, width), f32),
            jax.ShapeDtypeStruct((1, width), f32),
        ),
        in_specs=[vmem],
        out_specs=(vmem, vmem, vmem),
        name="totals",
    )(parts)
    return (
        mixed.reshape(1, pairs, width),
        dweight.reshape(1, pixels, width),
        dembed,
        dquery.reshape(width),
    )


def solution(mesh):
    return jax.shard_map(
        on_device,
        mesh=mesh,
        in_specs=(
            P("dp", "var", None, None),
            P("dp", None),
            P(),
            P("var", None, None),
            P("var", None),
            P(),
            P(),
            P(),
            P("dp", "var", None),
        ),
        out_specs=(P("dp", "var", None), P("var", None, None), P("var", None), P()),
        check_vma=False,
    )
```

```python
import math

import jax
import jax.numpy as jnp
from jax import lax
from jax.experimental import pallas as pl
from jax.experimental.pallas import tpu as pltpu
from jax.sharding import PartitionSpec as P

HEADS = 16
LANES = 128
SPAN = 256

field_eps = 1e-05
key_eps = 1e-06
masked_low = -1e30

f32 = jnp.float32
bf16 = jnp.bfloat16


def params(mib):
    return pltpu.CompilerParams(vmem_limit_bytes=mib * 2**20)


def stats_kernel(
    fields_ref,
    weight_ref,
    embed_ref,
    presence_ref,
    slot_ref,
    query_ref,
    grad_ref,
    stats_ref,
    fields_out,
    weight_out,
    embed_out,
    presence_out,
    slot_out,
    query_out,
    grad_out,
    arrivals,
):
    moves = [
        pltpu.make_async_copy(source, target, arrivals.at[i])
        for i, (source, target) in enumerate(
            (
                (presence_ref, presence_out),
                (slot_ref, slot_out),
                (fields_ref, fields_out),
                (weight_ref, weight_out),
                (embed_ref, embed_out),
                (query_ref, query_out),
                (grad_ref, grad_out),
            )
        )
    ]
    for move in moves:
        move.start()
    lane = lax.broadcasted_iota(jnp.int32, stats_ref.shape, 1)
    moves[0].wait()
    moves[1].wait()
    slot = jnp.where(lane == lax.axis_index("var"), slot_out[...], 0)
    slot = jnp.sum(slot.astype(f32), axis=1, keepdims=True).astype(jnp.int32)
    flag = jnp.where(lane == slot, presence_out[...], 0).astype(f32)
    flag = jnp.sum(flag, axis=1, keepdims=True)
    moves[2].wait()
    values = fields_out[...].astype(f32)
    cells = values.shape[0] * values.shape[1]
    total = jnp.sum(jnp.sum(values, axis=0, keepdims=True), axis=1, keepdims=True)
    centered = values - total / cells
    squares = jnp.sum(jnp.sum(centered * centered, axis=0, keepdims=True), axis=1, keepdims=True)
    stats_ref[...] = jnp.where(lane == 0, total, jnp.where(lane == 1, squares, 1.0)) * flag
    for move in moves[3:]:
        move.wait()


def token_kernel(stats_ref, fields_ref, weight_ref, embed_ref, tokens_ref, normed_ref, rows):
    pixels, patches = fields_ref.shape
    cells = float(patches * pixels)
    groups = weight_ref.shape[1] // LANES
    samples = stats_ref.shape[0]
    sums = [stats_ref[b, :, 0:1] for b in range(samples)]
    flags = [stats_ref[b, :, 2:3] for b in range(samples)]
    cell_total = jnp.maximum(sum(flags[1:], flags[0]), 1.0) * cells
    mean = sum(sums[1:], sums[0]) / cell_total
    second = jnp.zeros_like(mean)
    for b in range(samples):
        shift = sums[b] / cells - mean
        second = second + stats_ref[b, :, 1:2] + flags[b] * cells * shift * shift
    scale = lax.rsqrt(second / cell_total + field_eps)
    normed = ((fields_ref[...].astype(f32) - mean) * scale).astype(bf16)
    tokens = lax.dot_general(
        normed, weight_ref[...], (((0,), (0,)), ((), ())), preferred_element_type=f32
    )
    tokens = tokens + embed_ref[...].astype(f32)
    for j in range(groups):
        rows[pl.ds(j, patches, stride=groups), :] = tokens[:, j * LANES : (j + 1) * LANES]
    tokens_ref[...] = rows[...].reshape(tokens_ref.shape).astype(bf16)
    row = lax.broadcasted_iota(jnp.int32, (normed_ref.shape[0] - pixels, patches), 0)
    padded = jnp.concatenate([normed.astype(f32), jnp.where(row == 0, 1.0, 0.0)], axis=0)
    row = lax.broadcasted_iota(jnp.int32, (patches, patches), 0)
    lane = lax.broadcasted_iota(jnp.int32, (patches, patches), 1)
    half = patches // 2
    source = jnp.where(lane < half, 2 * lane, 2 * (lane - half) + 1)
    order = jnp.where(row == source, 1.0, 0.0).astype(bf16)
    normed_ref[...] = jnp.dot(padded.astype(bf16), order, preferred_element_type=f32).astype(bf16)


def head_lanes(width):
    row = lax.broadcasted_iota(jnp.int32, (LANES, width), 0)
    lane = lax.broadcasted_iota(jnp.int32, (LANES, width), 1)
    head = lane // (width // HEADS)
    return jnp.where((row % HEADS == head) & (row < 3 * HEADS), 1.0, 0.0).astype(bf16)


def head_sums(values, sums_ref, first, slots, head_dim):
    for p in range(sums_ref.shape[0]):
        for i in range(0, values.shape[1], LANES):
            block = jnp.transpose(values[p * slots : (p + 1) * slots, i : i + LANES])
            for k in range(LANES // head_dim):
                head = (first + i) // head_dim + k
                sums_ref[p, head : head + 1, :] = jnp.sum(
                    block[k * head_dim : (k + 1) * head_dim], axis=0, keepdims=True
                )


def three_parts(values):
    high = values.astype(bf16).astype(f32)
    rest = values - high
    middle = rest.astype(bf16).astype(f32)
    empty = jnp.zeros((LANES - 3 * HEADS, values.shape[1]), f32)
    parts = jnp.concatenate([high, middle, rest - middle, empty], axis=0)
    return jnp.transpose(parts).astype(bf16)


def mix_kernel(
    presence_ref,
    slot_ref,
    recv_ref,
    key_ref,
    value_ref,
    query_ref,
    grad_ref,
    mixed_ref,
    send_ref,
    arrived,
    tokens,
    keys,
    values,
    key_grad,
    value_grad,
    leaving,
    squares,
    raw,
    attn_grad,
):
    slots, recv_rows, _ = recv_ref.shape
    width = key_ref.shape[0]
    groups = width // LANES
    send_rows = send_ref.shape[1]
    head_dim = width // HEADS
    score_scale = 1.0 / math.sqrt(head_dim)
    pairs = recv_rows // groups
    spans = [slice(c, c + SPAN) for c in range(0, width, SPAN)]
    halves = [slice(p * slots, (p + 1) * slots) for p in range(pairs)]

    arrived[...] = recv_ref[...].astype(f32).reshape(arrived.shape)
    for p in range(pairs):
        for j in range(groups):
            block = arrived[pl.ds(p * groups + j, slots, stride=recv_rows), :]
            tokens[halves[p], j * LANES : (j + 1) * LANES] = block.astype(bf16)

    row = lax.broadcasted_iota(jnp.int32, (LANES, slots), 0)
    lookup = jnp.where(row == slot_ref[...], 1.0, 0.0).astype(bf16)
    present = jnp.broadcast_to(presence_ref[...].astype(f32), (HEADS, LANES)).astype(bf16)
    valid = jnp.dot(present, lookup, preferred_element_type=f32) > 0.5

    query = query_ref[...]
    grad = grad_ref[...].astype(f32)
    spread = head_lanes(width)
    for span in spans:
        block = jnp.dot(tokens[...], key_ref[:, span], preferred_element_type=f32)
        keys[:, span] = block
        head_sums(block * block, squares, span.start, slots, head_dim)
        head_sums(block * query[:, span], raw, span.start, slots, head_dim)
    for span in spans:
        block = jnp.dot(tokens[...], value_ref[:, span], preferred_element_type=f32)
        values[:, span] = block
        block = jnp.concatenate([block[halves[p]] * grad[p : p + 1, span] for p in range(pairs)], axis=0)
        head_sums(block, attn_grad, span.start, slots, head_dim)

    attention_parts, along_parts, across_parts = [], [], []
    for p in range(pairs):
        ratio = lax.rsqrt(squares[p] * (1.0 / head_dim) + key_eps)
        scores = raw[p] * ratio * score_scale
        top = jnp.max(jnp.where(valid, scores, masked_low), axis=1, keepdims=True)
        weights = jnp.where(valid, jnp.exp(scores - top), 0.0)
        weights = weights / jnp.sum(weights, axis=1, keepdims=True)
        change = attn_grad[p]
        inner = jnp.sum(weights * change, axis=1, keepdims=True)
        dscore = weights * (change - inner)
        attention_parts.append(three_parts(weights))
        along_parts.append(three_parts(dscore * ratio * score_scale))
        across_parts.append(three_parts(dscore * scores * ratio * ratio * (1.0 / head_dim)))
    attention_parts = jnp.concatenate(attention_parts, axis=0)
    along_parts = jnp.concatenate(along_parts, axis=0)
    across_parts = jnp.concatenate(across_parts, axis=0)

    for span in spans:
        weights = jnp.dot(attention_parts, spread[:, span], preferred_element_type=f32)
        first = jnp.dot(along_parts, spread[:, span], preferred_element_type=f32)
        second = jnp.dot(across_parts, spread[:, span], preferred_element_type=f32)
        key_block = keys[:, span]
        key_grad[:, span] = (first * query[:, span] - second * key_block).astype(bf16)
        dquery = jnp.sum(first * key_block, axis=0, keepdims=True)
        for p in range(pairs):
            part = weights[halves[p]]
            value_grad[halves[p], span] = (part * grad[p : p + 1, span]).astype(bf16)
            mixed_ref[p : p + 1, span] = jnp.sum(
                part * values[halves[p], span], axis=0, keepdims=True
            ).astype(bf16)
        for i in range(SPAN // LANES):
            j = span.start // LANES + i
            line = dquery[:, i * LANES : (i + 1) * LANES]
            leaving[pl.ds(pairs * groups + j, slots, stride=send_rows), :] = jnp.broadcast_to(
                line, (slots, LANES)
            )

    contract = (((1,), (1,)), ((), ()))
    for span in spans:
        block = lax.dot_general(key_grad[...], key_ref[span, :], contract, preferred_element_type=f32)
        block = block + lax.dot_general(
            value_grad[...], value_ref[span, :], contract, preferred_element_type=f32
        )
        for p in range(pairs):
            for i in range(SPAN // LANES):
                j = span.start // LANES + i
                leaving[pl.ds(p * groups + j, slots, stride=send_rows), :] = block[
                    halves[p], i * LANES : (i + 1) * LANES
                ]
    send_ref[...] = leaving[...].reshape(send_ref.shape).astype(bf16)


def mix_scratch(pairs, slots, width, rows, groups):
    return [
        pltpu.VMEM((slots * rows, LANES), f32),
        pltpu.VMEM((pairs * slots, width), bf16),
        pltpu.VMEM((pairs * slots, width), f32),
        pltpu.VMEM((pairs * slots, width), f32),
        pltpu.VMEM((pairs * slots, width), bf16),
        pltpu.VMEM((pairs * slots, width), bf16),
        pltpu.VMEM((slots * (rows + groups), LANES), f32),
        pltpu.VMEM((pairs, HEADS, slots), f32),
        pltpu.VMEM((pairs, HEADS, slots), f32),
        pltpu.VMEM((pairs, HEADS, slots), f32),
    ]


def grad_kernel(recv_ref, normed_ref, out_ref, arrived, grads):
    owners, recv_rows, _ = recv_ref.shape
    width = grads.shape[1]
    groups = width // LANES
    pairs = recv_rows // groups - 1
    copies, out_rows, _ = out_ref.shape
    pixels = out_rows // groups - 2
    blocks = recv_ref[...].astype(f32)
    arrived[...] = blocks.reshape(arrived.shape)
    dquery = jnp.sum(blocks[:, pairs * groups :, :], axis=0)
    for p in range(pairs):
        for j in range(groups):
            block = arrived[pl.ds(p * groups + j, owners, stride=recv_rows), :]
            grads[p * owners : (p + 1) * owners, j * LANES : (j + 1) * LANES] = block.astype(bf16)
    sums = jnp.dot(normed_ref[...], grads[...], preferred_element_type=f32)
    for j in range(groups):
        lanes = slice(j * LANES, (j + 1) * LANES)
        for c in range(copies):
            out_ref[c, j * pixels : (j + 1) * pixels, :] = sums[:pixels, lanes]
            out_ref[c, groups * pixels + j : groups * pixels + j + 1, :] = sums[
                pixels : pixels + 1, lanes
            ]
    for c in range(copies):
        out_ref[c, groups * (pixels + 1) :, :] = dquery


def total_kernel(parts_ref, weight_ref, embed_ref, query_ref):
    pixels, width = weight_ref.shape
    groups = width // LANES
    total = (parts_ref[0] + parts_ref[1]) + (parts_ref[2] + parts_ref[3])
    for j in range(groups):
        lanes = slice(j * LANES, (j + 1) * LANES)
        weight_ref[:, lanes] = total[j * pixels : (j + 1) * pixels]
        embed_ref[:, lanes] = total[groups * pixels + j : groups * pixels + j + 1]
        query_ref[:, lanes] = total[groups * (pixels + 1) + j : groups * (pixels + 1) + j + 1]


vmem = pl.BlockSpec(memory_space=pltpu.VMEM)
hbm = pl.BlockSpec(memory_space=pltpu.HBM)


def on_device(
    fields, presence, slot_var, patch_weight, var_embed, query, key_weight, value_weight, out_grad
):
    var_count = lax.axis_size("var")
    _, _, patches, pixels = fields.shape
    width = key_weight.shape[0]
    groups = width // LANES
    slots = slot_var.shape[0]
    pairs = patches // var_count
    rows = pairs * groups
    samples = lax.axis_size("dp")
    fixed = tuple(
        pltpu.with_memory_space_constraint(a, pltpu.HBM)
        for a in (
            jnp.transpose(fields.reshape(patches, pixels)),
        patch_weight.reshape(pixels, width),
        var_embed,
        presence,
        slot_var.reshape(1, slots),
        query.reshape(1, width),
        out_grad.reshape(pairs, width),
        )
    )

    stats, fields, patch_weight, var_embed, present, slot_row, query_row, grad_rows = pl.pallas_call(
        stats_kernel,
        out_shape=(pltpu.VMEM((1, LANES), f32),)
        + tuple(pltpu.VMEM(a.shape, a.dtype) for a in fixed),
        in_specs=[hbm] * len(fixed),
        out_specs=[vmem] * (1 + len(fixed)),
        scratch_shapes=[pltpu.SemaphoreType.DMA((len(fixed),))],
        name="stats",
    )(*fixed)
    stats = lax.all_gather(stats, "dp")

    tokens, normed = pl.pallas_call(
        token_kernel,
        out_shape=(
            jax.ShapeDtypeStruct((var_count, rows, LANES), bf16),
            jax.ShapeDtypeStruct((2 * pixels, patches), bf16),
        ),
        in_specs=[vmem] * 4,
        out_specs=(vmem, vmem),
        scratch_shapes=[pltpu.VMEM((patches * groups, LANES), f32)],
        compiler_params=params(16),
        cost_estimate=pl.CostEstimate(flops=6 * 10**9, bytes_accessed=2 * 10**6, transcendentals=0),
        name="tokens",
    )(stats, fields, patch_weight, var_embed)
    gathered = lax.all_to_all(tokens, "var", split_axis=0, concat_axis=0, tiled=True)

    mixed, outgoing = pl.pallas_call(
        mix_kernel,
        out_shape=(
            jax.ShapeDtypeStruct((pairs, width), bf16),
            jax.ShapeDtypeStruct((slots, rows + groups, LANES), bf16),
        ),
        in_specs=[vmem] * 7,
        out_specs=(vmem, vmem),
        scratch_shapes=mix_scratch(pairs, slots, width, rows, groups),
        compiler_params=params(32),
        name="mix",
    )(present, slot_row, gathered, key_weight, value_weight, query_row, grad_rows)
    returned = lax.all_to_all(outgoing, "var", split_axis=0, concat_axis=0, tiled=True)

    parts = pl.pallas_call(
        grad_kernel,
        out_shape=jax.ShapeDtypeStruct((samples, groups * (pixels + 2), LANES), f32),
        in_specs=[vmem, vmem],
        out_specs=vmem,
        scratch_shapes=[
            pltpu.VMEM((var_count * (rows + groups), LANES), f32),
            pltpu.VMEM((patches, width), bf16),
        ],
        compiler_params=params(16),
        name="grads",
    )(returned, normed)
    parts = lax.all_to_all(parts, "dp", split_axis=0, concat_axis=0, tiled=True)

    dweight, dembed, dquery = pl.pallas_call(
        total_kernel,
        out_shape=(
            jax.ShapeDtypeStruct((pixels, width), f32),
            jax.ShapeDtypeStruct((1, width), f32),
            jax.ShapeDtypeStruct((1, width), f32),
        ),
        in_specs=[vmem],
        out_specs=(vmem, vmem, vmem),
        compiler_params=params(16),
        name="totals",
    )(parts)
    return (
        mixed.reshape(1, pairs, width),
        dweight.reshape(1, pixels, width),
        dembed,
        dquery.reshape(width),
    )


def solution(mesh):
    return jax.shard_map(
        on_device,
        mesh=mesh,
        in_specs=(
            P("dp", "var", None, None),
            P("dp", None),
            P(),
            P("var", None, None),
            P("var", None),
            P(),
            P(),
            P(),
            P("dp", "var", None),
        ),
        out_specs=(P("dp", "var", None), P("var", None, None), P("var", None), P()),
        check_vma=False,
    )
```

```python
import math

import jax
import jax.numpy as jnp
from jax import lax
from jax.experimental import pallas as pl
from jax.experimental.pallas import tpu as pltpu
from jax.sharding import PartitionSpec as P

HEADS = 16
LANES = 128
SPAN = 256

field_eps = 1e-05
key_eps = 1e-06
masked_low = -1e30

f32 = jnp.float32
bf16 = jnp.bfloat16


def params(mib):
    return pltpu.CompilerParams(vmem_limit_bytes=mib * 2**20)


def stats_kernel(
    fields_ref,
    weight_ref,
    embed_ref,
    presence_ref,
    slot_ref,
    query_ref,
    grad_ref,
    stats_ref,
    fields_out,
    weight_out,
    embed_out,
    presence_out,
    slot_out,
    query_out,
    grad_out,
    arrivals,
):
    moves = [
        pltpu.make_async_copy(source, target, arrivals.at[i])
        for i, (source, target) in enumerate(
            (
                (presence_ref, presence_out),
                (slot_ref, slot_out),
                (fields_ref, fields_out),
                (weight_ref, weight_out),
                (embed_ref, embed_out),
                (query_ref, query_out),
                (grad_ref, grad_out),
            )
        )
    ]
    for move in moves:
        move.start()
    lane = lax.broadcasted_iota(jnp.int32, stats_ref.shape, 1)
    moves[0].wait()
    moves[1].wait()
    slot = jnp.where(lane == lax.axis_index("var"), slot_out[...], 0)
    slot = jnp.sum(slot.astype(f32), axis=1, keepdims=True).astype(jnp.int32)
    flag = jnp.where(lane == slot, presence_out[...], 0).astype(f32)
    flag = jnp.sum(flag, axis=1, keepdims=True)
    moves[2].wait()
    values = fields_out[...].astype(f32)
    cells = values.shape[0] * values.shape[1]
    total = jnp.sum(jnp.sum(values, axis=0, keepdims=True), axis=1, keepdims=True)
    centered = values - total / cells
    squares = jnp.sum(jnp.sum(centered * centered, axis=0, keepdims=True), axis=1, keepdims=True)
    stats_ref[...] = jnp.where(lane == 0, total, jnp.where(lane == 1, squares, 1.0)) * flag
    for move in moves[3:]:
        move.wait()


def token_kernel(stats_ref, fields_ref, weight_ref, embed_ref, tokens_ref, normed_ref, rows):
    pixels, patches = fields_ref.shape
    cells = float(patches * pixels)
    groups = weight_ref.shape[1] // LANES
    samples = stats_ref.shape[0]
    sums = [stats_ref[b, :, 0:1] for b in range(samples)]
    flags = [stats_ref[b, :, 2:3] for b in range(samples)]
    cell_total = jnp.maximum(sum(flags[1:], flags[0]), 1.0) * cells
    mean = sum(sums[1:], sums[0]) / cell_total
    second = jnp.zeros_like(mean)
    for b in range(samples):
        shift = sums[b] / cells - mean
        second = second + stats_ref[b, :, 1:2] + flags[b] * cells * shift * shift
    scale = lax.rsqrt(second / cell_total + field_eps)
    normed = ((fields_ref[...].astype(f32) - mean) * scale).astype(bf16)
    tokens = lax.dot_general(
        normed, weight_ref[...], (((0,), (0,)), ((), ())), preferred_element_type=f32
    )
    tokens = tokens + embed_ref[...].astype(f32)
    for j in range(groups):
        rows[pl.ds(j, patches, stride=groups), :] = tokens[:, j * LANES : (j + 1) * LANES]
    tokens_ref[...] = rows[...].reshape(tokens_ref.shape).astype(bf16)
    row = lax.broadcasted_iota(jnp.int32, (normed_ref.shape[0] - pixels, patches), 0)
    padded = jnp.concatenate([normed.astype(f32), jnp.where(row == 0, 1.0, 0.0)], axis=0)
    row = lax.broadcasted_iota(jnp.int32, (patches, patches), 0)
    lane = lax.broadcasted_iota(jnp.int32, (patches, patches), 1)
    half = patches // 2
    source = jnp.where(lane < half, 2 * lane, 2 * (lane - half) + 1)
    order = jnp.where(row == source, 1.0, 0.0).astype(bf16)
    normed_ref[...] = jnp.dot(padded.astype(bf16), order, preferred_element_type=f32).astype(bf16)


def head_lanes(width):
    row = lax.broadcasted_iota(jnp.int32, (LANES, width), 0)
    lane = lax.broadcasted_iota(jnp.int32, (LANES, width), 1)
    head = lane // (width // HEADS)
    return jnp.where((row % HEADS == head) & (row < 3 * HEADS), 1.0, 0.0).astype(bf16)


def head_sums(values, sums_ref, first, slots, head_dim):
    for p in range(sums_ref.shape[0]):
        for i in range(0, values.shape[1], LANES):
            block = jnp.transpose(values[p * slots : (p + 1) * slots, i : i + LANES])
            for k in range(LANES // head_dim):
                head = (first + i) // head_dim + k
                sums_ref[p, head : head + 1, :] = jnp.sum(
                    block[k * head_dim : (k + 1) * head_dim], axis=0, keepdims=True
                )


def three_parts(values):
    high = values.astype(bf16).astype(f32)
    rest = values - high
    middle = rest.astype(bf16).astype(f32)
    empty = jnp.zeros((LANES - 3 * HEADS, values.shape[1]), f32)
    parts = jnp.concatenate([high, middle, rest - middle, empty], axis=0)
    return jnp.transpose(parts).astype(bf16)


def mix_kernel(
    presence_ref,
    slot_ref,
    recv_ref,
    key_ref,
    value_ref,
    query_ref,
    grad_ref,
    mixed_ref,
    send_ref,
    arrived,
    tokens,
    keys,
    values,
    key_grad,
    value_grad,
    leaving,
    squares,
    raw,
    attn_grad,
):
    slots, recv_rows, _ = recv_ref.shape
    width = key_ref.shape[0]
    groups = width // LANES
    send_rows = send_ref.shape[1]
    head_dim = width // HEADS
    score_scale = 1.0 / math.sqrt(head_dim)
    pairs = recv_rows // groups
    spans = [slice(c, c + SPAN) for c in range(0, width, SPAN)]
    halves = [slice(p * slots, (p + 1) * slots) for p in range(pairs)]

    arrived[...] = recv_ref[...].astype(f32).reshape(arrived.shape)
    for p in range(pairs):
        for j in range(groups):
            block = arrived[pl.ds(p * groups + j, slots, stride=recv_rows), :]
            tokens[halves[p], j * LANES : (j + 1) * LANES] = block.astype(bf16)

    row = lax.broadcasted_iota(jnp.int32, (LANES, slots), 0)
    lookup = jnp.where(row == slot_ref[...], 1.0, 0.0).astype(bf16)
    present = jnp.broadcast_to(presence_ref[...].astype(f32), (HEADS, LANES)).astype(bf16)
    valid = jnp.dot(present, lookup, preferred_element_type=f32) > 0.5

    query = query_ref[...]
    grad = grad_ref[...].astype(f32)
    spread = head_lanes(width)
    for span in spans:
        block = jnp.dot(tokens[...], key_ref[:, span], preferred_element_type=f32)
        keys[:, span] = block
        head_sums(block * block, squares, span.start, slots, head_dim)
        head_sums(block * query[:, span], raw, span.start, slots, head_dim)
    for span in spans:
        block = jnp.dot(tokens[...], value_ref[:, span], preferred_element_type=f32)
        values[:, span] = block
        block = jnp.concatenate([block[halves[p]] * grad[p : p + 1, span] for p in range(pairs)], axis=0)
        head_sums(block, attn_grad, span.start, slots, head_dim)

    attention_parts, along_parts, across_parts = [], [], []
    for p in range(pairs):
        ratio = lax.rsqrt(squares[p] * (1.0 / head_dim) + key_eps)
        scores = raw[p] * ratio * score_scale
        top = jnp.max(jnp.where(valid, scores, masked_low), axis=1, keepdims=True)
        weights = jnp.where(valid, jnp.exp(scores - top), 0.0)
        weights = weights / jnp.sum(weights, axis=1, keepdims=True)
        change = attn_grad[p]
        inner = jnp.sum(weights * change, axis=1, keepdims=True)
        dscore = weights * (change - inner)
        attention_parts.append(three_parts(weights))
        along_parts.append(three_parts(dscore * ratio * score_scale))
        across_parts.append(three_parts(dscore * scores * ratio * ratio * (1.0 / head_dim)))
    attention_parts = jnp.concatenate(attention_parts, axis=0)
    along_parts = jnp.concatenate(along_parts, axis=0)
    across_parts = jnp.concatenate(across_parts, axis=0)

    for span in spans:
        weights = jnp.dot(attention_parts, spread[:, span], preferred_element_type=f32)
        first = jnp.dot(along_parts, spread[:, span], preferred_element_type=f32)
        second = jnp.dot(across_parts, spread[:, span], preferred_element_type=f32)
        key_block = keys[:, span]
        key_grad[:, span] = (first * query[:, span] - second * key_block).astype(bf16)
        dquery = jnp.sum(first * key_block, axis=0, keepdims=True)
        for p in range(pairs):
            part = weights[halves[p]]
            value_grad[halves[p], span] = (part * grad[p : p + 1, span]).astype(bf16)
            mixed_ref[p : p + 1, span] = jnp.sum(
                part * values[halves[p], span], axis=0, keepdims=True
            ).astype(bf16)
        for i in range(SPAN // LANES):
            j = span.start // LANES + i
            line = dquery[:, i * LANES : (i + 1) * LANES]
            leaving[pl.ds(pairs * groups + j, slots, stride=send_rows), :] = jnp.broadcast_to(
                line, (slots, LANES)
            )

    contract = (((1,), (1,)), ((), ()))
    for span in spans:
        block = lax.dot_general(key_grad[...], key_ref[span, :], contract, preferred_element_type=f32)
        block = block + lax.dot_general(
            value_grad[...], value_ref[span, :], contract, preferred_element_type=f32
        )
        for p in range(pairs):
            for i in range(SPAN // LANES):
                j = span.start // LANES + i
                leaving[pl.ds(p * groups + j, slots, stride=send_rows), :] = block[
                    halves[p], i * LANES : (i + 1) * LANES
                ]
    send_ref[...] = leaving[...].reshape(send_ref.shape).astype(bf16)


def mix_scratch(pairs, slots, width, rows, groups):
    return [
        pltpu.VMEM((slots * rows, LANES), f32),
        pltpu.VMEM((pairs * slots, width), bf16),
        pltpu.VMEM((pairs * slots, width), f32),
        pltpu.VMEM((pairs * slots, width), f32),
        pltpu.VMEM((pairs * slots, width), bf16),
        pltpu.VMEM((pairs * slots, width), bf16),
        pltpu.VMEM((slots * (rows + groups), LANES), f32),
        pltpu.VMEM((pairs, HEADS, slots), f32),
        pltpu.VMEM((pairs, HEADS, slots), f32),
        pltpu.VMEM((pairs, HEADS, slots), f32),
    ]


def grad_kernel(recv_ref, normed_ref, out_ref, arrived, grads, packed):
    owners, recv_rows, _ = recv_ref.shape
    width = grads.shape[1]
    groups = width // LANES
    pairs = recv_rows // groups - 1
    copies, out_rows, _ = out_ref.shape
    pixels = out_rows // groups - 2
    blocks = recv_ref[...].astype(f32)
    arrived[...] = blocks.reshape(arrived.shape)
    dquery = jnp.sum(blocks[:, pairs * groups :, :], axis=0)
    for p in range(pairs):
        for j in range(groups):
            block = arrived[pl.ds(p * groups + j, owners, stride=recv_rows), :]
            grads[p * owners : (p + 1) * owners, j * LANES : (j + 1) * LANES] = block.astype(bf16)
    sums = jnp.dot(normed_ref[...], grads[...], preferred_element_type=f32)
    for j in range(groups):
        lanes = slice(j * LANES, (j + 1) * LANES)
        packed[j * pixels : (j + 1) * pixels, :] = sums[:pixels, lanes]
        packed[groups * pixels + j : groups * pixels + j + 1, :] = sums[pixels : pixels + 1, lanes]
    packed[groups * (pixels + 1) :, :] = dquery
    total = packed[...].astype(bf16)
    for c in range(copies):
        out_ref[c] = total


def total_kernel(parts_ref, weight_ref, embed_ref, query_ref):
    pixels, width = weight_ref.shape
    groups = width // LANES
    parts = [parts_ref[b].astype(f32) for b in range(parts_ref.shape[0])]
    total = sum(parts[1:], parts[0])
    for j in range(groups):
        lanes = slice(j * LANES, (j + 1) * LANES)
        weight_ref[:, lanes] = total[j * pixels : (j + 1) * pixels]
        embed_ref[:, lanes] = total[groups * pixels + j : groups * pixels + j + 1]
        query_ref[:, lanes] = total[groups * (pixels + 1) + j : groups * (pixels + 1) + j + 1]


vmem = pl.BlockSpec(memory_space=pltpu.VMEM)
hbm = pl.BlockSpec(memory_space=pltpu.HBM)


def on_device(
    fields, presence, slot_var, patch_weight, var_embed, query, key_weight, value_weight, out_grad
):
    var_count = lax.axis_size("var")
    _, _, patches, pixels = fields.shape
    width = key_weight.shape[0]
    groups = width // LANES
    slots = slot_var.shape[0]
    pairs = patches // var_count
    rows = pairs * groups
    samples = lax.axis_size("dp")
    fixed = tuple(
        pltpu.with_memory_space_constraint(a, pltpu.HBM)
        for a in (
            jnp.transpose(fields.reshape(patches, pixels)),
        patch_weight.reshape(pixels, width),
        var_embed,
        presence,
        slot_var.reshape(1, slots),
        query.reshape(1, width),
        out_grad.reshape(pairs, width),
        )
    )

    stats, fields, patch_weight, var_embed, present, slot_row, query_row, grad_rows = pl.pallas_call(
        stats_kernel,
        out_shape=(pltpu.VMEM((1, LANES), f32),)
        + tuple(pltpu.VMEM(a.shape, a.dtype) for a in fixed),
        in_specs=[hbm] * len(fixed),
        out_specs=[vmem] * (1 + len(fixed)),
        scratch_shapes=[pltpu.SemaphoreType.DMA((len(fixed),))],
        name="stats",
    )(*fixed)
    stats = lax.all_gather(stats, "dp")

    tokens, normed = pl.pallas_call(
        token_kernel,
        out_shape=(
            jax.ShapeDtypeStruct((var_count, rows, LANES), bf16),
            jax.ShapeDtypeStruct((2 * pixels, patches), bf16),
        ),
        in_specs=[vmem] * 4,
        out_specs=(vmem, vmem),
        scratch_shapes=[pltpu.VMEM((patches * groups, LANES), f32)],
        compiler_params=params(16),
        cost_estimate=pl.CostEstimate(flops=6 * 10**9, bytes_accessed=2 * 10**6, transcendentals=0),
        name="tokens",
    )(stats, fields, patch_weight, var_embed)
    gathered = lax.all_to_all(tokens, "var", split_axis=0, concat_axis=0, tiled=True)

    mixed, outgoing = pl.pallas_call(
        mix_kernel,
        out_shape=(
            jax.ShapeDtypeStruct((pairs, width), bf16),
            jax.ShapeDtypeStruct((slots, rows + groups, LANES), bf16),
        ),
        in_specs=[vmem] * 7,
        out_specs=(vmem, vmem),
        scratch_shapes=mix_scratch(pairs, slots, width, rows, groups),
        compiler_params=params(32),
        name="mix",
    )(present, slot_row, gathered, key_weight, value_weight, query_row, grad_rows)
    returned = lax.all_to_all(outgoing, "var", split_axis=0, concat_axis=0, tiled=True)

    parts = pl.pallas_call(
        grad_kernel,
        out_shape=jax.ShapeDtypeStruct((samples, groups * (pixels + 2), LANES), bf16),
        in_specs=[vmem, vmem],
        out_specs=vmem,
        scratch_shapes=[
            pltpu.VMEM((var_count * (rows + groups), LANES), f32),
            pltpu.VMEM((patches, width), bf16),
            pltpu.VMEM((groups * (pixels + 2), LANES), f32),
        ],
        compiler_params=params(16),
        name="grads",
    )(returned, normed)
    parts = lax.all_to_all(parts, "dp", split_axis=0, concat_axis=0, tiled=True)

    dweight, dembed, dquery = pl.pallas_call(
        total_kernel,
        out_shape=(
            jax.ShapeDtypeStruct((pixels, width), f32),
            jax.ShapeDtypeStruct((1, width), f32),
            jax.ShapeDtypeStruct((1, width), f32),
        ),
        in_specs=[vmem],
        out_specs=(vmem, vmem, vmem),
        compiler_params=params(16),
        name="totals",
    )(parts)
    return (
        mixed.reshape(1, pairs, width),
        dweight.reshape(1, pixels, width),
        dembed,
        dquery.reshape(width),
    )


def solution(mesh):
    return jax.shard_map(
        on_device,
        mesh=mesh,
        in_specs=(
            P("dp", "var", None, None),
            P("dp", None),
            P(),
            P("var", None, None),
            P("var", None),
            P(),
            P(),
            P(),
            P("dp", "var", None),
        ),
        out_specs=(P("dp", "var", None), P("var", None, None), P("var", None), P()),
        check_vma=False,
    )
```

```python
import math

import jax
import jax.numpy as jnp
from jax import lax
from jax.experimental import pallas as pl
from jax.experimental.pallas import tpu as pltpu
from jax.sharding import PartitionSpec as P

HEADS = 16
LANES = 128
SPAN = 256

field_eps = 1e-05
key_eps = 1e-06
masked_low = -1e30

f32 = jnp.float32
bf16 = jnp.bfloat16


def params(mib):
    return pltpu.CompilerParams(vmem_limit_bytes=mib * 2**20)


def stats_kernel(
    fields_ref,
    weight_ref,
    embed_ref,
    presence_ref,
    slot_ref,
    query_ref,
    grad_ref,
    stats_ref,
    fields_out,
    weight_out,
    embed_out,
    presence_out,
    slot_out,
    query_out,
    grad_out,
    arrivals,
):
    moves = [
        pltpu.make_async_copy(source, target, arrivals.at[i])
        for i, (source, target) in enumerate(
            (
                (presence_ref, presence_out),
                (slot_ref, slot_out),
                (fields_ref, fields_out),
                (weight_ref, weight_out),
                (embed_ref, embed_out),
                (query_ref, query_out),
                (grad_ref, grad_out),
            )
        )
    ]
    for move in moves:
        move.start()
    lane = lax.broadcasted_iota(jnp.int32, stats_ref.shape, 1)
    for move in moves[:3]:
        move.wait()
    slot = jnp.where(lane == lax.axis_index("var"), slot_out[...], 0)
    slot = jnp.sum(slot.astype(f32), axis=1, keepdims=True).astype(jnp.int32)
    flag = jnp.where(lane == slot, presence_out[...], 0).astype(f32)
    flag = jnp.sum(flag, axis=1, keepdims=True)
    values = fields_out[...].astype(f32)
    cells = values.shape[0] * values.shape[1]
    total = jnp.sum(jnp.sum(values, axis=0, keepdims=True), axis=1, keepdims=True)
    centered = values - total / cells
    squares = jnp.sum(jnp.sum(centered * centered, axis=0, keepdims=True), axis=1, keepdims=True)
    stats = jnp.where(lane == 0, total, jnp.where(lane == 1, squares, 1.0))
    stats_ref[...] = jnp.where(flag > 0.5, stats, 0.0)
    for move in moves[3:]:
        move.wait()


def token_kernel(stats_ref, fields_ref, weight_ref, embed_ref, tokens_ref, normed_ref, rows):
    pixels, patches = fields_ref.shape
    cells = float(patches * pixels)
    groups = weight_ref.shape[1] // LANES
    samples = stats_ref.shape[0]
    sums = [stats_ref[b, :, 0:1] for b in range(samples)]
    flags = [stats_ref[b, :, 2:3] for b in range(samples)]
    cell_total = jnp.maximum(sum(flags[1:], flags[0]), 1.0) * cells
    mean = sum(sums[1:], sums[0]) / cell_total
    second = jnp.zeros_like(mean)
    for b in range(samples):
        shift = sums[b] / cells - mean
        second = second + stats_ref[b, :, 1:2] + flags[b] * cells * shift * shift
    scale = lax.rsqrt(second / cell_total + field_eps)
    normed = ((fields_ref[...].astype(f32) - mean) * scale).astype(bf16)
    tokens = lax.dot_general(
        normed, weight_ref[...], (((0,), (0,)), ((), ())), preferred_element_type=f32
    )
    tokens = tokens + embed_ref[...].astype(f32)
    for j in range(groups):
        rows[pl.ds(j, patches, stride=groups), :] = tokens[:, j * LANES : (j + 1) * LANES]
    tokens_ref[...] = rows[...].reshape(tokens_ref.shape).astype(bf16)
    row = lax.broadcasted_iota(jnp.int32, (normed_ref.shape[0] - pixels, patches), 0)
    padded = jnp.concatenate([normed.astype(f32), jnp.where(row == 0, 1.0, 0.0)], axis=0)
    row = lax.broadcasted_iota(jnp.int32, (patches, patches), 0)
    lane = lax.broadcasted_iota(jnp.int32, (patches, patches), 1)
    half = patches // 2
    source = jnp.where(lane < half, 2 * lane, 2 * (lane - half) + 1)
    order = jnp.where(row == source, 1.0, 0.0).astype(bf16)
    normed_ref[...] = jnp.dot(padded.astype(bf16), order, preferred_element_type=f32).astype(bf16)


def head_lanes(width):
    row = lax.broadcasted_iota(jnp.int32, (LANES, width), 0)
    lane = lax.broadcasted_iota(jnp.int32, (LANES, width), 1)
    head = lane // (width // HEADS)
    return jnp.where((row % HEADS == head) & (row < 3 * HEADS), 1.0, 0.0).astype(bf16)


def head_sums(values, sums_ref, first, slots, head_dim):
    for p in range(sums_ref.shape[0]):
        for i in range(0, values.shape[1], LANES):
            block = jnp.transpose(values[p * slots : (p + 1) * slots, i : i + LANES])
            for k in range(LANES // head_dim):
                head = (first + i) // head_dim + k
                sums_ref[p, head : head + 1, :] = jnp.sum(
                    block[k * head_dim : (k + 1) * head_dim], axis=0, keepdims=True
                )


def three_parts(values):
    high = values.astype(bf16).astype(f32)
    rest = values - high
    middle = rest.astype(bf16).astype(f32)
    empty = jnp.zeros((LANES - 3 * HEADS, values.shape[1]), f32)
    parts = jnp.concatenate([high, middle, rest - middle, empty], axis=0)
    return jnp.transpose(parts).astype(bf16)


def mix_kernel(
    presence_ref,
    slot_ref,
    recv_ref,
    key_ref,
    value_ref,
    query_ref,
    grad_ref,
    mixed_ref,
    send_ref,
    arrived,
    tokens,
    keys,
    values,
    key_grad,
    value_grad,
    leaving,
    squares,
    raw,
    attn_grad,
):
    slots, recv_rows, _ = recv_ref.shape
    width = key_ref.shape[0]
    groups = width // LANES
    send_rows = send_ref.shape[1]
    head_dim = width // HEADS
    score_scale = 1.0 / math.sqrt(head_dim)
    pairs = recv_rows // groups
    spans = [slice(c, c + SPAN) for c in range(0, width, SPAN)]
    halves = [slice(p * slots, (p + 1) * slots) for p in range(pairs)]

    arrived[...] = recv_ref[...].astype(f32).reshape(arrived.shape)
    for p in range(pairs):
        for j in range(groups):
            block = arrived[pl.ds(p * groups + j, slots, stride=recv_rows), :]
            tokens[halves[p], j * LANES : (j + 1) * LANES] = block.astype(bf16)

    row = lax.broadcasted_iota(jnp.int32, (LANES, slots), 0)
    lookup = jnp.where(row == slot_ref[...], 1.0, 0.0).astype(bf16)
    present = jnp.broadcast_to(presence_ref[...].astype(f32), (HEADS, LANES)).astype(bf16)
    valid = jnp.dot(present, lookup, preferred_element_type=f32) > 0.5

    query = query_ref[...]
    grad = grad_ref[...].astype(f32)
    spread = head_lanes(width)
    for span in spans:
        block = jnp.dot(tokens[...], key_ref[:, span], preferred_element_type=f32)
        keys[:, span] = block
        head_sums(block * block, squares, span.start, slots, head_dim)
        head_sums(block * query[:, span], raw, span.start, slots, head_dim)
    for span in spans:
        block = jnp.dot(tokens[...], value_ref[:, span], preferred_element_type=f32)
        values[:, span] = block
        block = jnp.concatenate([block[halves[p]] * grad[p : p + 1, span] for p in range(pairs)], axis=0)
        head_sums(block, attn_grad, span.start, slots, head_dim)

    attention_parts, along_parts, across_parts = [], [], []
    for p in range(pairs):
        ratio = lax.rsqrt(squares[p] * (1.0 / head_dim) + key_eps)
        scores = raw[p] * ratio * score_scale
        top = jnp.max(jnp.where(valid, scores, masked_low), axis=1, keepdims=True)
        weights = jnp.where(valid, jnp.exp(scores - top), 0.0)
        weights = weights / jnp.sum(weights, axis=1, keepdims=True)
        change = attn_grad[p]
        inner = jnp.sum(weights * change, axis=1, keepdims=True)
        dscore = weights * (change - inner)
        attention_parts.append(three_parts(weights))
        along_parts.append(three_parts(dscore * ratio * score_scale))
        across_parts.append(three_parts(dscore * scores * ratio * ratio * (1.0 / head_dim)))
    attention_parts = jnp.concatenate(attention_parts, axis=0)
    along_parts = jnp.concatenate(along_parts, axis=0)
    across_parts = jnp.concatenate(across_parts, axis=0)

    for span in spans:
        weights = jnp.dot(attention_parts, spread[:, span], preferred_element_type=f32)
        first = jnp.dot(along_parts, spread[:, span], preferred_element_type=f32)
        second = jnp.dot(across_parts, spread[:, span], preferred_element_type=f32)
        key_block = keys[:, span]
        key_grad[:, span] = (first * query[:, span] - second * key_block).astype(bf16)
        dquery = jnp.sum(first * key_block, axis=0, keepdims=True)
        for p in range(pairs):
            part = weights[halves[p]]
            value_grad[halves[p], span] = (part * grad[p : p + 1, span]).astype(bf16)
            mixed_ref[p : p + 1, span] = jnp.sum(
                part * values[halves[p], span], axis=0, keepdims=True
            ).astype(bf16)
        for i in range(SPAN // LANES):
            j = span.start // LANES + i
            line = dquery[:, i * LANES : (i + 1) * LANES]
            leaving[pl.ds(pairs * groups + j, slots, stride=send_rows), :] = jnp.broadcast_to(
                line, (slots, LANES)
            )

    contract = (((1,), (1,)), ((), ()))
    for span in spans:
        block = lax.dot_general(key_grad[...], key_ref[span, :], contract, preferred_element_type=f32)
        block = block + lax.dot_general(
            value_grad[...], value_ref[span, :], contract, preferred_element_type=f32
        )
        for p in range(pairs):
            for i in range(SPAN // LANES):
                j = span.start // LANES + i
                leaving[pl.ds(p * groups + j, slots, stride=send_rows), :] = block[
                    halves[p], i * LANES : (i + 1) * LANES
                ]
    send_ref[...] = leaving[...].reshape(send_ref.shape).astype(bf16)


def mix_scratch(pairs, slots, width, rows, groups):
    return [
        pltpu.VMEM((slots * rows, LANES), f32),
        pltpu.VMEM((pairs * slots, width), bf16),
        pltpu.VMEM((pairs * slots, width), f32),
        pltpu.VMEM((pairs * slots, width), f32),
        pltpu.VMEM((pairs * slots, width), bf16),
        pltpu.VMEM((pairs * slots, width), bf16),
        pltpu.VMEM((slots * (rows + groups), LANES), f32),
        pltpu.VMEM((pairs, HEADS, slots), f32),
        pltpu.VMEM((pairs, HEADS, slots), f32),
        pltpu.VMEM((pairs, HEADS, slots), f32),
    ]


def grad_kernel(recv_ref, normed_ref, out_ref, arrived, grads, packed):
    owners, recv_rows, _ = recv_ref.shape
    width = grads.shape[1]
    groups = width // LANES
    pairs = recv_rows // groups - 1
    copies, out_rows, _ = out_ref.shape
    pixels = out_rows // groups - 2
    blocks = recv_ref[...].astype(f32)
    arrived[...] = blocks.reshape(arrived.shape)
    dquery = jnp.sum(blocks[:, pairs * groups :, :], axis=0)
    for p in range(pairs):
        for j in range(groups):
            block = arrived[pl.ds(p * groups + j, owners, stride=recv_rows), :]
            grads[p * owners : (p + 1) * owners, j * LANES : (j + 1) * LANES] = block.astype(bf16)
    sums = jnp.dot(normed_ref[...], grads[...], preferred_element_type=f32)
    for j in range(groups):
        lanes = slice(j * LANES, (j + 1) * LANES)
        packed[j * pixels : (j + 1) * pixels, :] = sums[:pixels, lanes]
        packed[groups * pixels + j : groups * pixels + j + 1, :] = sums[pixels : pixels + 1, lanes]
    packed[groups * (pixels + 1) :, :] = dquery
    total = packed[...].astype(bf16)
    for c in range(copies):
        out_ref[c] = total


def total_kernel(parts_ref, weight_ref, embed_ref, query_ref):
    pixels, width = weight_ref.shape
    groups = width // LANES
    parts = [parts_ref[b].astype(f32) for b in range(parts_ref.shape[0])]
    total = sum(parts[1:], parts[0])
    for j in range(groups):
        lanes = slice(j * LANES, (j + 1) * LANES)
        weight_ref[:, lanes] = total[j * pixels : (j + 1) * pixels]
        embed_ref[:, lanes] = total[groups * pixels + j : groups * pixels + j + 1]
        query_ref[:, lanes] = total[groups * (pixels + 1) + j : groups * (pixels + 1) + j + 1]


vmem = pl.BlockSpec(memory_space=pltpu.VMEM)
hbm = pl.BlockSpec(memory_space=pltpu.HBM)


def on_device(
    fields, presence, slot_var, patch_weight, var_embed, query, key_weight, value_weight, out_grad
):
    var_count = lax.axis_size("var")
    _, _, patches, pixels = fields.shape
    width = key_weight.shape[0]
    groups = width // LANES
    slots = slot_var.shape[0]
    pairs = patches // var_count
    rows = pairs * groups
    samples = lax.axis_size("dp")
    fixed = tuple(
        pltpu.with_memory_space_constraint(a, pltpu.HBM)
        for a in (
            jnp.transpose(fields.reshape(patches, pixels)),
        patch_weight.reshape(pixels, width),
        var_embed,
        presence,
        slot_var.reshape(1, slots),
        query.reshape(1, width),
        out_grad.reshape(pairs, width),
        )
    )

    stats, fields, patch_weight, var_embed, present, slot_row, query_row, grad_rows = pl.pallas_call(
        stats_kernel,
        out_shape=(pltpu.VMEM((1, LANES), f32),)
        + tuple(pltpu.VMEM(a.shape, a.dtype) for a in fixed),
        in_specs=[hbm] * len(fixed),
        out_specs=[vmem] * (1 + len(fixed)),
        scratch_shapes=[pltpu.SemaphoreType.DMA((len(fixed),))],
        name="stats",
    )(*fixed)
    stats = lax.all_gather(stats, "dp")

    tokens, normed = pl.pallas_call(
        token_kernel,
        out_shape=(
            jax.ShapeDtypeStruct((var_count, rows, LANES), bf16),
            jax.ShapeDtypeStruct((2 * pixels, patches), bf16),
        ),
        in_specs=[vmem] * 4,
        out_specs=(vmem, vmem),
        scratch_shapes=[pltpu.VMEM((patches * groups, LANES), f32)],
        compiler_params=params(16),
        cost_estimate=pl.CostEstimate(flops=6 * 10**9, bytes_accessed=2 * 10**6, transcendentals=0),
        name="tokens",
    )(stats, fields, patch_weight, var_embed)
    gathered = lax.all_to_all(tokens, "var", split_axis=0, concat_axis=0, tiled=True)

    mixed, outgoing = pl.pallas_call(
        mix_kernel,
        out_shape=(
            jax.ShapeDtypeStruct((pairs, width), bf16),
            jax.ShapeDtypeStruct((slots, rows + groups, LANES), bf16),
        ),
        in_specs=[vmem] * 7,
        out_specs=(vmem, vmem),
        scratch_shapes=mix_scratch(pairs, slots, width, rows, groups),
        compiler_params=params(32),
        name="mix",
    )(present, slot_row, gathered, key_weight, value_weight, query_row, grad_rows)
    returned = lax.all_to_all(outgoing, "var", split_axis=0, concat_axis=0, tiled=True)

    parts = pl.pallas_call(
        grad_kernel,
        out_shape=jax.ShapeDtypeStruct((samples, groups * (pixels + 2), LANES), bf16),
        in_specs=[vmem, vmem],
        out_specs=vmem,
        scratch_shapes=[
            pltpu.VMEM((var_count * (rows + groups), LANES), f32),
            pltpu.VMEM((patches, width), bf16),
            pltpu.VMEM((groups * (pixels + 2), LANES), f32),
        ],
        compiler_params=params(16),
        name="grads",
    )(returned, normed)
    parts = lax.all_to_all(parts, "dp", split_axis=0, concat_axis=0, tiled=True)

    dweight, dembed, dquery = pl.pallas_call(
        total_kernel,
        out_shape=(
            jax.ShapeDtypeStruct((pixels, width), f32),
            jax.ShapeDtypeStruct((1, width), f32),
            jax.ShapeDtypeStruct((1, width), f32),
        ),
        in_specs=[vmem],
        out_specs=(vmem, vmem, vmem),
        compiler_params=params(16),
        name="totals",
    )(parts)
    return (
        mixed.reshape(1, pairs, width),
        dweight.reshape(1, pixels, width),
        dembed,
        dquery.reshape(width),
    )


def solution(mesh):
    return jax.shard_map(
        on_device,
        mesh=mesh,
        in_specs=(
            P("dp", "var", None, None),
            P("dp", None),
            P(),
            P("var", None, None),
            P("var", None),
            P(),
            P(),
            P(),
            P("dp", "var", None),
        ),
        out_specs=(P("dp", "var", None), P("var", None, None), P("var", None), P()),
        check_vma=False,
    )
```

```python
import math

import jax
import jax.numpy as jnp
from jax import lax
from jax.experimental import pallas as pl
from jax.experimental.pallas import tpu as pltpu
from jax.sharding import PartitionSpec as P

HEADS = 16
LANES = 128
TURNS = 4
SPAN = 256

field_eps = 1e-05
key_eps = 1e-06
masked_low = -1e30

f32 = jnp.float32
bf16 = jnp.bfloat16


def params(mib):
    return pltpu.CompilerParams(vmem_limit_bytes=mib * 2**20)


def stats_kernel(
    fields_ref,
    weight_ref,
    embed_ref,
    presence_ref,
    slot_ref,
    query_ref,
    grad_ref,
    stats_ref,
    fields_out,
    weight_out,
    embed_out,
    presence_out,
    slot_out,
    query_out,
    grad_out,
    arrivals,
):
    moves = [
        pltpu.make_async_copy(source, target, arrivals.at[i])
        for i, (source, target) in enumerate(
            (
                (presence_ref, presence_out),
                (slot_ref, slot_out),
                (fields_ref, fields_out),
                (weight_ref, weight_out),
                (embed_ref, embed_out),
                (query_ref, query_out),
                (grad_ref, grad_out),
            )
        )
    ]
    for move in moves:
        move.start()
    lane = lax.broadcasted_iota(jnp.int32, stats_ref.shape, 1)
    for move in moves[:3]:
        move.wait()
    slot = jnp.where(lane == lax.axis_index("var"), slot_out[...], 0)
    slot = jnp.sum(slot.astype(f32), axis=1, keepdims=True).astype(jnp.int32)
    flag = jnp.where(lane == slot, presence_out[...], 0).astype(f32)
    flag = jnp.sum(flag, axis=1, keepdims=True)
    values = fields_out[...].astype(f32)
    cells = values.shape[0] * values.shape[1]
    total = jnp.sum(jnp.sum(values, axis=0, keepdims=True), axis=1, keepdims=True)
    centered = values - total / cells
    squares = jnp.sum(jnp.sum(centered * centered, axis=0, keepdims=True), axis=1, keepdims=True)
    turn = lane % TURNS
    stats = jnp.where(turn == 0, total, jnp.where(turn == 1, squares, 1.0))
    stats_ref[...] = jnp.where(flag > 0.5, stats, 0.0)
    for move in moves[3:]:
        move.wait()


def token_kernel(stats_ref, fields_ref, weight_ref, embed_ref, tokens_ref, normed_ref, rows):
    pixels, patches = fields_ref.shape
    cells = float(patches * pixels)
    groups = weight_ref.shape[1] // LANES
    samples = stats_ref.shape[0]
    lane = lax.broadcasted_iota(jnp.int32, (1, LANES), 1)
    sums, squares, flags = [], [], []
    for b in range(samples):
        turned = [stats_ref[b]]
        turned.extend(pltpu.roll(turned[0], k, 1) for k in range(1, TURNS))
        for which, out in enumerate((sums, squares, flags)):
            value = turned[0]
            for k in range(1, TURNS):
                value = jnp.where((lane + (TURNS - which)) % TURNS == k, turned[k], value)
            out.append(value)
    cell_total = jnp.maximum(sum(flags[1:], flags[0]), 1.0) * cells
    mean = sum(sums[1:], sums[0]) / cell_total
    second = jnp.zeros_like(mean)
    for b in range(samples):
        shift = sums[b] / cells - mean
        second = second + squares[b] + flags[b] * cells * shift * shift
    scale = lax.rsqrt(second / cell_total + field_eps)
    mean, scale = (jnp.concatenate([x] * (patches // LANES), axis=1) for x in (mean, scale))
    normed = ((fields_ref[...].astype(f32) - mean) * scale).astype(bf16)
    tokens = lax.dot_general(
        normed, weight_ref[...], (((0,), (0,)), ((), ())), preferred_element_type=f32
    )
    tokens = tokens + embed_ref[...].astype(f32)
    for j in range(groups):
        rows[pl.ds(j, patches, stride=groups), :] = tokens[:, j * LANES : (j + 1) * LANES]
    tokens_ref[...] = rows[...].reshape(tokens_ref.shape).astype(bf16)
    row = lax.broadcasted_iota(jnp.int32, (normed_ref.shape[0] - pixels, patches), 0)
    padded = jnp.concatenate([normed.astype(f32), jnp.where(row == 0, 1.0, 0.0)], axis=0)
    row = lax.broadcasted_iota(jnp.int32, (patches, patches), 0)
    lane = lax.broadcasted_iota(jnp.int32, (patches, patches), 1)
    half = patches // 2
    source = jnp.where(lane < half, 2 * lane, 2 * (lane - half) + 1)
    order = jnp.where(row == source, 1.0, 0.0).astype(bf16)
    normed_ref[...] = jnp.dot(padded.astype(bf16), order, preferred_element_type=f32).astype(bf16)


def head_lanes(width):
    row = lax.broadcasted_iota(jnp.int32, (LANES, width), 0)
    lane = lax.broadcasted_iota(jnp.int32, (LANES, width), 1)
    head = lane // (width // HEADS)
    return jnp.where((row % HEADS == head) & (row < 3 * HEADS), 1.0, 0.0).astype(bf16)


def head_sums(values, sums_ref, first, slots, head_dim):
    for p in range(sums_ref.shape[0]):
        for i in range(0, values.shape[1], LANES):
            block = jnp.transpose(values[p * slots : (p + 1) * slots, i : i + LANES])
            for k in range(LANES // head_dim):
                head = (first + i) // head_dim + k
                sums_ref[p, head : head + 1, :] = jnp.sum(
                    block[k * head_dim : (k + 1) * head_dim], axis=0, keepdims=True
                )


def three_parts(values):
    high = values.astype(bf16).astype(f32)
    rest = values - high
    middle = rest.astype(bf16).astype(f32)
    empty = jnp.zeros((LANES - 3 * HEADS, values.shape[1]), f32)
    parts = jnp.concatenate([high, middle, rest - middle, empty], axis=0)
    return jnp.transpose(parts).astype(bf16)


def mix_kernel(
    presence_ref,
    slot_ref,
    recv_ref,
    key_ref,
    value_ref,
    query_ref,
    grad_ref,
    mixed_ref,
    send_ref,
    arrived,
    tokens,
    keys,
    values,
    key_grad,
    value_grad,
    leaving,
    squares,
    raw,
    attn_grad,
):
    slots, recv_rows, _ = recv_ref.shape
    width = key_ref.shape[0]
    groups = width // LANES
    send_rows = send_ref.shape[1]
    head_dim = width // HEADS
    score_scale = 1.0 / math.sqrt(head_dim)
    pairs = recv_rows // groups
    spans = [slice(c, c + SPAN) for c in range(0, width, SPAN)]
    halves = [slice(p * slots, (p + 1) * slots) for p in range(pairs)]

    arrived[...] = recv_ref[...].astype(f32).reshape(arrived.shape)
    for p in range(pairs):
        for j in range(groups):
            block = arrived[pl.ds(p * groups + j, slots, stride=recv_rows), :]
            tokens[halves[p], j * LANES : (j + 1) * LANES] = block.astype(bf16)

    row = lax.broadcasted_iota(jnp.int32, (LANES, slots), 0)
    lookup = jnp.where(row == slot_ref[...], 1.0, 0.0).astype(bf16)
    present = jnp.broadcast_to(presence_ref[...].astype(f32), (HEADS, LANES)).astype(bf16)
    valid = jnp.dot(present, lookup, preferred_element_type=f32) > 0.5

    query = query_ref[...]
    grad = grad_ref[...].astype(f32)
    spread = head_lanes(width)
    for span in spans:
        block = jnp.dot(tokens[...], key_ref[:, span], preferred_element_type=f32)
        keys[:, span] = block
        head_sums(block * block, squares, span.start, slots, head_dim)
        head_sums(block * query[:, span], raw, span.start, slots, head_dim)
    for span in spans:
        block = jnp.dot(tokens[...], value_ref[:, span], preferred_element_type=f32)
        values[:, span] = block
        block = jnp.concatenate([block[halves[p]] * grad[p : p + 1, span] for p in range(pairs)], axis=0)
        head_sums(block, attn_grad, span.start, slots, head_dim)

    attention_parts, along_parts, across_parts = [], [], []
    for p in range(pairs):
        ratio = lax.rsqrt(squares[p] * (1.0 / head_dim) + key_eps)
        scores = raw[p] * ratio * score_scale
        top = jnp.max(jnp.where(valid, scores, masked_low), axis=1, keepdims=True)
        weights = jnp.where(valid, jnp.exp(scores - top), 0.0)
        weights = weights / jnp.sum(weights, axis=1, keepdims=True)
        change = attn_grad[p]
        inner = jnp.sum(weights * change, axis=1, keepdims=True)
        dscore = weights * (change - inner)
        attention_parts.append(three_parts(weights))
        along_parts.append(three_parts(dscore * ratio * score_scale))
        across_parts.append(three_parts(dscore * scores * ratio * ratio * (1.0 / head_dim)))
    attention_parts = jnp.concatenate(attention_parts, axis=0)
    along_parts = jnp.concatenate(along_parts, axis=0)
    across_parts = jnp.concatenate(across_parts, axis=0)

    for span in spans:
        weights = jnp.dot(attention_parts, spread[:, span], preferred_element_type=f32)
        first = jnp.dot(along_parts, spread[:, span], preferred_element_type=f32)
        second = jnp.dot(across_parts, spread[:, span], preferred_element_type=f32)
        key_block = keys[:, span]
        key_grad[:, span] = (first * query[:, span] - second * key_block).astype(bf16)
        dquery = jnp.sum(first * key_block, axis=0, keepdims=True)
        for p in range(pairs):
            part = weights[halves[p]]
            value_grad[halves[p], span] = (part * grad[p : p + 1, span]).astype(bf16)
            mixed_ref[p : p + 1, span] = jnp.sum(
                part * values[halves[p], span], axis=0, keepdims=True
            ).astype(bf16)
        for i in range(SPAN // LANES):
            j = span.start // LANES + i
            line = dquery[:, i * LANES : (i + 1) * LANES]
            leaving[pl.ds(pairs * groups + j, slots, stride=send_rows), :] = jnp.broadcast_to(
                line, (slots, LANES)
            )

    contract = (((1,), (1,)), ((), ()))
    for span in spans:
        block = lax.dot_general(key_grad[...], key_ref[span, :], contract, preferred_element_type=f32)
        block = block + lax.dot_general(
            value_grad[...], value_ref[span, :], contract, preferred_element_type=f32
        )
        for p in range(pairs):
            for i in range(SPAN // LANES):
                j = span.start // LANES + i
                leaving[pl.ds(p * groups + j, slots, stride=send_rows), :] = block[
                    halves[p], i * LANES : (i + 1) * LANES
                ]
    send_ref[...] = leaving[...].reshape(send_ref.shape).astype(bf16)


def mix_scratch(pairs, slots, width, rows, groups):
    return [
        pltpu.VMEM((slots * rows, LANES), f32),
        pltpu.VMEM((pairs * slots, width), bf16),
        pltpu.VMEM((pairs * slots, width), f32),
        pltpu.VMEM((pairs * slots, width), f32),
        pltpu.VMEM((pairs * slots, width), bf16),
        pltpu.VMEM((pairs * slots, width), bf16),
        pltpu.VMEM((slots * (rows + groups), LANES), f32),
        pltpu.VMEM((pairs, HEADS, slots), f32),
        pltpu.VMEM((pairs, HEADS, slots), f32),
        pltpu.VMEM((pairs, HEADS, slots), f32),
    ]


def grad_kernel(recv_ref, normed_ref, out_ref, arrived, grads, packed):
    owners, recv_rows, _ = recv_ref.shape
    width = grads.shape[1]
    groups = width // LANES
    pairs = recv_rows // groups - 1
    copies, out_rows, _ = out_ref.shape
    pixels = out_rows // groups - 2
    blocks = recv_ref[...].astype(f32)
    arrived[...] = blocks.reshape(arrived.shape)
    dquery = jnp.sum(blocks[:, pairs * groups :, :], axis=0)
    for p in range(pairs):
        for j in range(groups):
            block = arrived[pl.ds(p * groups + j, owners, stride=recv_rows), :]
            grads[p * owners : (p + 1) * owners, j * LANES : (j + 1) * LANES] = block.astype(bf16)
    sums = jnp.dot(normed_ref[...], grads[...], preferred_element_type=f32)
    for j in range(groups):
        lanes = slice(j * LANES, (j + 1) * LANES)
        packed[j * pixels : (j + 1) * pixels, :] = sums[:pixels, lanes]
        packed[groups * pixels + j : groups * pixels + j + 1, :] = sums[pixels : pixels + 1, lanes]
    packed[groups * (pixels + 1) :, :] = dquery
    total = packed[...].astype(bf16)
    for c in range(copies):
        out_ref[c] = total


def total_kernel(parts_ref, weight_ref, embed_ref, query_ref):
    pixels, width = weight_ref.shape
    groups = width // LANES
    parts = [parts_ref[b].astype(f32) for b in range(parts_ref.shape[0])]
    total = sum(parts[1:], parts[0])
    for j in range(groups):
        lanes = slice(j * LANES, (j + 1) * LANES)
        weight_ref[:, lanes] = total[j * pixels : (j + 1) * pixels]
        embed_ref[:, lanes] = total[groups * pixels + j : groups * pixels + j + 1]
        query_ref[:, lanes] = total[groups * (pixels + 1) + j : groups * (pixels + 1) + j + 1]


vmem = pl.BlockSpec(memory_space=pltpu.VMEM)
hbm = pl.BlockSpec(memory_space=pltpu.HBM)


def on_device(
    fields, presence, slot_var, patch_weight, var_embed, query, key_weight, value_weight, out_grad
):
    var_count = lax.axis_size("var")
    _, _, patches, pixels = fields.shape
    width = key_weight.shape[0]
    groups = width // LANES
    slots = slot_var.shape[0]
    pairs = patches // var_count
    rows = pairs * groups
    samples = lax.axis_size("dp")
    fixed = tuple(
        pltpu.with_memory_space_constraint(a, pltpu.HBM)
        for a in (
            jnp.transpose(fields.reshape(patches, pixels)),
        patch_weight.reshape(pixels, width),
        var_embed,
        presence,
        slot_var.reshape(1, slots),
        query.reshape(1, width),
        out_grad.reshape(pairs, width),
        )
    )

    stats, fields, patch_weight, var_embed, present, slot_row, query_row, grad_rows = pl.pallas_call(
        stats_kernel,
        out_shape=(pltpu.VMEM((1, LANES), f32),)
        + tuple(pltpu.VMEM(a.shape, a.dtype) for a in fixed),
        in_specs=[hbm] * len(fixed),
        out_specs=[vmem] * (1 + len(fixed)),
        scratch_shapes=[pltpu.SemaphoreType.DMA((len(fixed),))],
        name="stats",
    )(*fixed)
    stats = lax.all_gather(stats, "dp")

    tokens, normed = pl.pallas_call(
        token_kernel,
        out_shape=(
            jax.ShapeDtypeStruct((var_count, rows, LANES), bf16),
            jax.ShapeDtypeStruct((2 * pixels, patches), bf16),
        ),
        in_specs=[vmem] * 4,
        out_specs=(vmem, vmem),
        scratch_shapes=[pltpu.VMEM((patches * groups, LANES), f32)],
        compiler_params=params(16),
        cost_estimate=pl.CostEstimate(flops=6 * 10**9, bytes_accessed=2 * 10**6, transcendentals=0),
        name="tokens",
    )(stats, fields, patch_weight, var_embed)
    gathered = lax.all_to_all(tokens, "var", split_axis=0, concat_axis=0, tiled=True)

    mixed, outgoing = pl.pallas_call(
        mix_kernel,
        out_shape=(
            jax.ShapeDtypeStruct((pairs, width), bf16),
            jax.ShapeDtypeStruct((slots, rows + groups, LANES), bf16),
        ),
        in_specs=[vmem] * 7,
        out_specs=(vmem, vmem),
        scratch_shapes=mix_scratch(pairs, slots, width, rows, groups),
        compiler_params=params(32),
        name="mix",
    )(present, slot_row, gathered, key_weight, value_weight, query_row, grad_rows)
    returned = lax.all_to_all(outgoing, "var", split_axis=0, concat_axis=0, tiled=True)

    parts = pl.pallas_call(
        grad_kernel,
        out_shape=jax.ShapeDtypeStruct((samples, groups * (pixels + 2), LANES), bf16),
        in_specs=[vmem, vmem],
        out_specs=vmem,
        scratch_shapes=[
            pltpu.VMEM((var_count * (rows + groups), LANES), f32),
            pltpu.VMEM((patches, width), bf16),
            pltpu.VMEM((groups * (pixels + 2), LANES), f32),
        ],
        compiler_params=params(16),
        name="grads",
    )(returned, normed)
    parts = lax.all_to_all(parts, "dp", split_axis=0, concat_axis=0, tiled=True)

    dweight, dembed, dquery = pl.pallas_call(
        total_kernel,
        out_shape=(
            jax.ShapeDtypeStruct((pixels, width), f32),
            jax.ShapeDtypeStruct((1, width), f32),
            jax.ShapeDtypeStruct((1, width), f32),
        ),
        in_specs=[vmem],
        out_specs=(vmem, vmem, vmem),
        compiler_params=params(16),
        name="totals",
    )(parts)
    return (
        mixed.reshape(1, pairs, width),
        dweight.reshape(1, pixels, width),
        dembed,
        dquery.reshape(width),
    )


def solution(mesh):
    return jax.shard_map(
        on_device,
        mesh=mesh,
        in_specs=(
            P("dp", "var", None, None),
            P("dp", None),
            P(),
            P("var", None, None),
            P("var", None),
            P(),
            P(),
            P(),
            P("dp", "var", None),
        ),
        out_specs=(P("dp", "var", None), P("var", None, None), P("var", None), P()),
        check_vma=False,
    )
```

```python
import math

import jax
import jax.numpy as jnp
from jax import lax
from jax.experimental import pallas as pl
from jax.experimental.pallas import tpu as pltpu
from jax.sharding import PartitionSpec as P

HEADS = 16
LANES = 128
TURNS = 4
SPAN = 1024

field_eps = 1e-05
key_eps = 1e-06
masked_low = -1e30

f32 = jnp.float32
bf16 = jnp.bfloat16


def params(mib):
    return pltpu.CompilerParams(vmem_limit_bytes=mib * 2**20)


def stats_kernel(
    fields_ref,
    weight_ref,
    embed_ref,
    presence_ref,
    slot_ref,
    query_ref,
    grad_ref,
    stats_ref,
    fields_out,
    weight_out,
    embed_out,
    presence_out,
    slot_out,
    query_out,
    grad_out,
    arrivals,
):
    moves = [
        pltpu.make_async_copy(source, target, arrivals.at[i])
        for i, (source, target) in enumerate(
            (
                (presence_ref, presence_out),
                (slot_ref, slot_out),
                (fields_ref, fields_out),
                (weight_ref, weight_out),
                (embed_ref, embed_out),
                (query_ref, query_out),
                (grad_ref, grad_out),
            )
        )
    ]
    for move in moves:
        move.start()
    lane = lax.broadcasted_iota(jnp.int32, stats_ref.shape, 1)
    for move in moves[:3]:
        move.wait()
    slot = jnp.where(lane == lax.axis_index("var"), slot_out[...], 0)
    slot = jnp.sum(slot.astype(f32), axis=1, keepdims=True).astype(jnp.int32)
    flag = jnp.where(lane == slot, presence_out[...], 0).astype(f32)
    flag = jnp.sum(flag, axis=1, keepdims=True)
    values = fields_out[...].astype(f32)
    cells = values.shape[0] * values.shape[1]
    total = jnp.sum(jnp.sum(values, axis=0, keepdims=True), axis=1, keepdims=True)
    centered = values - total / cells
    squares = jnp.sum(jnp.sum(centered * centered, axis=0, keepdims=True), axis=1, keepdims=True)
    turn = lane % TURNS
    stats = jnp.where(turn == 0, total, jnp.where(turn == 1, squares, 1.0))
    stats_ref[...] = jnp.where(flag > 0.5, stats, 0.0)
    for move in moves[3:]:
        move.wait()


def token_kernel(stats_ref, fields_ref, weight_ref, embed_ref, tokens_ref, normed_ref, rows):
    pixels, patches = fields_ref.shape
    cells = float(patches * pixels)
    groups = weight_ref.shape[1] // LANES
    samples = stats_ref.shape[0]
    lane = lax.broadcasted_iota(jnp.int32, (1, LANES), 1)
    sums, squares, flags = [], [], []
    for b in range(samples):
        turned = [stats_ref[b]]
        turned.extend(pltpu.roll(turned[0], k, 1) for k in range(1, TURNS))
        for which, out in enumerate((sums, squares, flags)):
            value = turned[0]
            for k in range(1, TURNS):
                value = jnp.where((lane + (TURNS - which)) % TURNS == k, turned[k], value)
            out.append(value)
    cell_total = jnp.maximum(sum(flags[1:], flags[0]), 1.0) * cells
    mean = sum(sums[1:], sums[0]) / cell_total
    second = jnp.zeros_like(mean)
    for b in range(samples):
        shift = sums[b] / cells - mean
        second = second + squares[b] + flags[b] * cells * shift * shift
    scale = lax.rsqrt(second / cell_total + field_eps)
    mean, scale = (jnp.concatenate([x] * (patches // LANES), axis=1) for x in (mean, scale))
    normed = ((fields_ref[...].astype(f32) - mean) * scale).astype(bf16)
    tokens = lax.dot_general(
        normed, weight_ref[...], (((0,), (0,)), ((), ())), preferred_element_type=f32
    )
    tokens = tokens + embed_ref[...].astype(f32)
    for j in range(groups):
        rows[pl.ds(j, patches, stride=groups), :] = tokens[:, j * LANES : (j + 1) * LANES]
    tokens_ref[...] = rows[...].reshape(tokens_ref.shape).astype(bf16)
    row = lax.broadcasted_iota(jnp.int32, (normed_ref.shape[0] - pixels, patches), 0)
    padded = jnp.concatenate([normed.astype(f32), jnp.where(row == 0, 1.0, 0.0)], axis=0)
    row = lax.broadcasted_iota(jnp.int32, (patches, patches), 0)
    lane = lax.broadcasted_iota(jnp.int32, (patches, patches), 1)
    half = patches // 2
    source = jnp.where(lane < half, 2 * lane, 2 * (lane - half) + 1)
    order = jnp.where(row == source, 1.0, 0.0).astype(bf16)
    normed_ref[...] = jnp.dot(padded.astype(bf16), order, preferred_element_type=f32).astype(bf16)


def head_lanes(width):
    row = lax.broadcasted_iota(jnp.int32, (LANES, width), 0)
    lane = lax.broadcasted_iota(jnp.int32, (LANES, width), 1)
    head = lane // (width // HEADS)
    return jnp.where((row % HEADS == head) & (row < 3 * HEADS), 1.0, 0.0).astype(bf16)


def head_sums(values, sums_ref, first, slots, head_dim):
    for p in range(sums_ref.shape[0]):
        for i in range(0, values.shape[1], LANES):
            block = jnp.transpose(values[p * slots : (p + 1) * slots, i : i + LANES])
            for k in range(LANES // head_dim):
                head = (first + i) // head_dim + k
                sums_ref[p, head : head + 1, :] = jnp.sum(
                    block[k * head_dim : (k + 1) * head_dim], axis=0, keepdims=True
                )


def three_parts(values):
    high = values.astype(bf16).astype(f32)
    rest = values - high
    middle = rest.astype(bf16).astype(f32)
    empty = jnp.zeros((LANES - 3 * HEADS, values.shape[1]), f32)
    parts = jnp.concatenate([high, middle, rest - middle, empty], axis=0)
    return jnp.transpose(parts).astype(bf16)


def mix_kernel(
    presence_ref,
    slot_ref,
    recv_ref,
    key_ref,
    value_ref,
    query_ref,
    grad_ref,
    mixed_ref,
    send_ref,
    arrived,
    tokens,
    keys,
    values,
    key_grad,
    value_grad,
    leaving,
    squares,
    raw,
    attn_grad,
):
    slots, recv_rows, _ = recv_ref.shape
    width = key_ref.shape[0]
    groups = width // LANES
    send_rows = send_ref.shape[1]
    head_dim = width // HEADS
    score_scale = 1.0 / math.sqrt(head_dim)
    pairs = recv_rows // groups
    spans = [slice(c, c + SPAN) for c in range(0, width, SPAN)]
    halves = [slice(p * slots, (p + 1) * slots) for p in range(pairs)]

    arrived[...] = recv_ref[...].astype(f32).reshape(arrived.shape)
    for p in range(pairs):
        for j in range(groups):
            block = arrived[pl.ds(p * groups + j, slots, stride=recv_rows), :]
            tokens[halves[p], j * LANES : (j + 1) * LANES] = block.astype(bf16)

    row = lax.broadcasted_iota(jnp.int32, (LANES, slots), 0)
    lookup = jnp.where(row == slot_ref[...], 1.0, 0.0).astype(bf16)
    present = jnp.broadcast_to(presence_ref[...].astype(f32), (HEADS, LANES)).astype(bf16)
    valid = jnp.dot(present, lookup, preferred_element_type=f32) > 0.5

    query = query_ref[...]
    grad = grad_ref[...].astype(f32)
    spread = head_lanes(width)
    for span in spans:
        block = jnp.dot(tokens[...], key_ref[:, span], preferred_element_type=f32)
        keys[:, span] = block
        head_sums(block * block, squares, span.start, slots, head_dim)
        head_sums(block * query[:, span], raw, span.start, slots, head_dim)
    for span in spans:
        block = jnp.dot(tokens[...], value_ref[:, span], preferred_element_type=f32)
        values[:, span] = block
        block = jnp.concatenate([block[halves[p]] * grad[p : p + 1, span] for p in range(pairs)], axis=0)
        head_sums(block, attn_grad, span.start, slots, head_dim)

    attention_parts, along_parts, across_parts = [], [], []
    for p in range(pairs):
        ratio = lax.rsqrt(squares[p] * (1.0 / head_dim) + key_eps)
        scores = raw[p] * ratio * score_scale
        top = jnp.max(jnp.where(valid, scores, masked_low), axis=1, keepdims=True)
        weights = jnp.where(valid, jnp.exp(scores - top), 0.0)
        change = attn_grad[p]
        inner = jnp.sum(weights * change, axis=1, keepdims=True)
        share = 1.0 / jnp.sum(weights, axis=1, keepdims=True)
        weights = weights * share
        inner = inner * share
        dscore = weights * (change - inner)
        attention_parts.append(three_parts(weights))
        along_parts.append(three_parts(dscore * ratio * score_scale))
        across_parts.append(three_parts(dscore * scores * ratio * ratio * (1.0 / head_dim)))
    attention_parts = jnp.concatenate(attention_parts, axis=0)
    along_parts = jnp.concatenate(along_parts, axis=0)
    across_parts = jnp.concatenate(across_parts, axis=0)

    for span in spans:
        weights = jnp.dot(attention_parts, spread[:, span], preferred_element_type=f32)
        first = jnp.dot(along_parts, spread[:, span], preferred_element_type=f32)
        second = jnp.dot(across_parts, spread[:, span], preferred_element_type=f32)
        key_block = keys[:, span]
        key_grad[:, span] = (first * query[:, span] - second * key_block).astype(bf16)
        dquery = jnp.sum(first * key_block, axis=0, keepdims=True)
        for p in range(pairs):
            part = weights[halves[p]]
            value_grad[halves[p], span] = (part * grad[p : p + 1, span]).astype(bf16)
            mixed_ref[p : p + 1, span] = jnp.sum(
                part * values[halves[p], span], axis=0, keepdims=True
            ).astype(bf16)
        for i in range(SPAN // LANES):
            j = span.start // LANES + i
            line = dquery[:, i * LANES : (i + 1) * LANES]
            leaving[pl.ds(pairs * groups + j, slots, stride=send_rows), :] = jnp.broadcast_to(
                line, (slots, LANES)
            )

    contract = (((1,), (1,)), ((), ()))
    for span in spans:
        block = lax.dot_general(key_grad[...], key_ref[span, :], contract, preferred_element_type=f32)
        block = block + lax.dot_general(
            value_grad[...], value_ref[span, :], contract, preferred_element_type=f32
        )
        for p in range(pairs):
            for i in range(SPAN // LANES):
                j = span.start // LANES + i
                leaving[pl.ds(p * groups + j, slots, stride=send_rows), :] = block[
                    halves[p], i * LANES : (i + 1) * LANES
                ]
    send_ref[...] = leaving[...].reshape(send_ref.shape).astype(bf16)


def mix_scratch(pairs, slots, width, rows, groups):
    return [
        pltpu.VMEM((slots * rows, LANES), f32),
        pltpu.VMEM((pairs * slots, width), bf16),
        pltpu.VMEM((pairs * slots, width), f32),
        pltpu.VMEM((pairs * slots, width), f32),
        pltpu.VMEM((pairs * slots, width), bf16),
        pltpu.VMEM((pairs * slots, width), bf16),
        pltpu.VMEM((slots * (rows + groups), LANES), f32),
        pltpu.VMEM((pairs, HEADS, slots), f32),
        pltpu.VMEM((pairs, HEADS, slots), f32),
        pltpu.VMEM((pairs, HEADS, slots), f32),
    ]


def grad_kernel(recv_ref, normed_ref, out_ref, arrived, grads, packed):
    owners, recv_rows, _ = recv_ref.shape
    width = grads.shape[1]
    groups = width // LANES
    pairs = recv_rows // groups - 1
    copies, out_rows, _ = out_ref.shape
    pixels = out_rows // groups - 2
    blocks = recv_ref[...].astype(f32)
    arrived[...] = blocks.reshape(arrived.shape)
    dquery = jnp.sum(blocks[:, pairs * groups :, :], axis=0)
    for p in range(pairs):
        for j in range(groups):
            block = arrived[pl.ds(p * groups + j, owners, stride=recv_rows), :]
            grads[p * owners : (p + 1) * owners, j * LANES : (j + 1) * LANES] = block.astype(bf16)
    sums = jnp.dot(normed_ref[...], grads[...], preferred_element_type=f32)
    for j in range(groups):
        lanes = slice(j * LANES, (j + 1) * LANES)
        packed[j * pixels : (j + 1) * pixels, :] = sums[:pixels, lanes]
        packed[groups * pixels + j : groups * pixels + j + 1, :] = sums[pixels : pixels + 1, lanes]
    packed[groups * (pixels + 1) :, :] = dquery
    total = packed[...].astype(bf16)
    for c in range(copies):
        out_ref[c] = total


def total_kernel(parts_ref, weight_ref, embed_ref, query_ref):
    pixels, width = weight_ref.shape
    groups = width // LANES
    parts = [parts_ref[b].astype(f32) for b in range(parts_ref.shape[0])]
    total = sum(parts[1:], parts[0])
    for j in range(groups):
        lanes = slice(j * LANES, (j + 1) * LANES)
        weight_ref[:, lanes] = total[j * pixels : (j + 1) * pixels]
        embed_ref[:, lanes] = total[groups * pixels + j : groups * pixels + j + 1]
        query_ref[:, lanes] = total[groups * (pixels + 1) + j : groups * (pixels + 1) + j + 1]


vmem = pl.BlockSpec(memory_space=pltpu.VMEM)
hbm = pl.BlockSpec(memory_space=pltpu.HBM)


def on_device(
    fields, presence, slot_var, patch_weight, var_embed, query, key_weight, value_weight, out_grad
):
    var_count = lax.axis_size("var")
    _, _, patches, pixels = fields.shape
    width = key_weight.shape[0]
    groups = width // LANES
    slots = slot_var.shape[0]
    pairs = patches // var_count
    rows = pairs * groups
    samples = lax.axis_size("dp")
    fixed = tuple(
        pltpu.with_memory_space_constraint(a, pltpu.HBM)
        for a in (
            jnp.transpose(fields.reshape(patches, pixels)),
        patch_weight.reshape(pixels, width),
        var_embed,
        presence,
        slot_var.reshape(1, slots),
        query.reshape(1, width),
        out_grad.reshape(pairs, width),
        )
    )

    stats, fields, patch_weight, var_embed, present, slot_row, query_row, grad_rows = pl.pallas_call(
        stats_kernel,
        out_shape=(pltpu.VMEM((1, LANES), f32),)
        + tuple(pltpu.VMEM(a.shape, a.dtype) for a in fixed),
        in_specs=[hbm] * len(fixed),
        out_specs=[vmem] * (1 + len(fixed)),
        scratch_shapes=[pltpu.SemaphoreType.DMA((len(fixed),))],
        name="stats",
    )(*fixed)
    stats = lax.all_gather(stats, "dp")

    tokens, normed = pl.pallas_call(
        token_kernel,
        out_shape=(
            jax.ShapeDtypeStruct((var_count, rows, LANES), bf16),
            jax.ShapeDtypeStruct((2 * pixels, patches), bf16),
        ),
        in_specs=[vmem] * 4,
        out_specs=(vmem, vmem),
        scratch_shapes=[pltpu.VMEM((patches * groups, LANES), f32)],
        compiler_params=params(16),
        cost_estimate=pl.CostEstimate(flops=6 * 10**9, bytes_accessed=2 * 10**6, transcendentals=0),
        name="tokens",
    )(stats, fields, patch_weight, var_embed)
    gathered = lax.all_to_all(tokens, "var", split_axis=0, concat_axis=0, tiled=True)

    mixed, outgoing = pl.pallas_call(
        mix_kernel,
        out_shape=(
            jax.ShapeDtypeStruct((pairs, width), bf16),
            jax.ShapeDtypeStruct((slots, rows + groups, LANES), bf16),
        ),
        in_specs=[vmem] * 7,
        out_specs=(vmem, vmem),
        scratch_shapes=mix_scratch(pairs, slots, width, rows, groups),
        compiler_params=params(32),
        name="mix",
    )(present, slot_row, gathered, key_weight, value_weight, query_row, grad_rows)
    returned = lax.all_to_all(outgoing, "var", split_axis=0, concat_axis=0, tiled=True)

    parts = pl.pallas_call(
        grad_kernel,
        out_shape=jax.ShapeDtypeStruct((samples, groups * (pixels + 2), LANES), bf16),
        in_specs=[vmem, vmem],
        out_specs=vmem,
        scratch_shapes=[
            pltpu.VMEM((var_count * (rows + groups), LANES), f32),
            pltpu.VMEM((patches, width), bf16),
            pltpu.VMEM((groups * (pixels + 2), LANES), f32),
        ],
        compiler_params=params(16),
        name="grads",
    )(returned, normed)
    parts = lax.all_to_all(parts, "dp", split_axis=0, concat_axis=0, tiled=True)

    dweight, dembed, dquery = pl.pallas_call(
        total_kernel,
        out_shape=(
            jax.ShapeDtypeStruct((pixels, width), f32),
            jax.ShapeDtypeStruct((1, width), f32),
            jax.ShapeDtypeStruct((1, width), f32),
        ),
        in_specs=[vmem],
        out_specs=(vmem, vmem, vmem),
        compiler_params=params(16),
        name="totals",
    )(parts)
    return (
        mixed.reshape(1, pairs, width),
        dweight.reshape(1, pixels, width),
        dembed,
        dquery.reshape(width),
    )


def solution(mesh):
    return jax.shard_map(
        on_device,
        mesh=mesh,
        in_specs=(
            P("dp", "var", None, None),
            P("dp", None),
            P(),
            P("var", None, None),
            P("var", None),
            P(),
            P(),
            P(),
            P("dp", "var", None),
        ),
        out_specs=(P("dp", "var", None), P("var", None, None), P("var", None), P()),
        check_vma=False,
    )
```

```python
import math

import jax
import jax.numpy as jnp
from jax import lax
from jax.experimental import pallas as pl
from jax.experimental.pallas import tpu as pltpu
from jax.sharding import PartitionSpec as P

HEADS = 16
LANES = 128
TURNS = 4
SPAN = 1024

field_eps = 1e-05
key_eps = 1e-06
masked_low = -1e30

f32 = jnp.float32
bf16 = jnp.bfloat16


def params(mib):
    return pltpu.CompilerParams(vmem_limit_bytes=mib * 2**20)


def stats_kernel(
    fields_ref,
    weight_ref,
    embed_ref,
    presence_ref,
    slot_ref,
    query_ref,
    grad_ref,
    stats_ref,
    fields_out,
    weight_out,
    embed_out,
    presence_out,
    slot_out,
    query_out,
    grad_out,
    arrivals,
):
    moves = [
        pltpu.make_async_copy(source, target, arrivals.at[i])
        for i, (source, target) in enumerate(
            (
                (presence_ref, presence_out),
                (slot_ref, slot_out),
                (fields_ref, fields_out),
                (weight_ref, weight_out),
                (embed_ref, embed_out),
                (query_ref, query_out),
                (grad_ref, grad_out),
            )
        )
    ]
    for move in moves:
        move.start()
    lane = lax.broadcasted_iota(jnp.int32, stats_ref.shape, 1)
    for move in moves[:3]:
        move.wait()
    slot = jnp.where(lane == lax.axis_index("var"), slot_out[...], 0)
    slot = jnp.sum(slot.astype(f32), axis=1, keepdims=True).astype(jnp.int32)
    flag = jnp.where(lane == slot, presence_out[...], 0).astype(f32)
    flag = jnp.sum(flag, axis=1, keepdims=True)
    values = fields_out[...].astype(f32)
    cells = values.shape[0] * values.shape[1]
    ones = jnp.ones((values.shape[1], LANES), bf16)
    total = jnp.dot(fields_out[...], ones, preferred_element_type=f32)
    total = jnp.sum(total, axis=0, keepdims=True)
    mean = jnp.concatenate([total / cells] * (values.shape[1] // LANES), axis=1)
    rest = (values - mean) * (values - mean)
    squares = jnp.zeros((values.shape[0], LANES), f32)
    for _ in range(3):
        part = rest.astype(bf16)
        squares = squares + jnp.dot(part, ones, preferred_element_type=f32)
        rest = rest - part.astype(f32)
    squares = jnp.sum(squares, axis=0, keepdims=True)
    turn = lane % TURNS
    stats = jnp.where(turn == 0, total, jnp.where(turn == 1, squares, 1.0))
    stats_ref[...] = jnp.where(flag > 0.5, stats, 0.0)
    for move in moves[3:]:
        move.wait()


def token_kernel(stats_ref, fields_ref, weight_ref, embed_ref, tokens_ref, normed_ref, rows):
    pixels, patches = fields_ref.shape
    cells = float(patches * pixels)
    groups = weight_ref.shape[1] // LANES
    samples = stats_ref.shape[0]
    lane = lax.broadcasted_iota(jnp.int32, (1, LANES), 1)
    sums, squares, flags = [], [], []
    for b in range(samples):
        turned = [stats_ref[b]]
        turned.extend(pltpu.roll(turned[0], k, 1) for k in range(1, TURNS))
        for which, out in enumerate((sums, squares, flags)):
            value = turned[0]
            for k in range(1, TURNS):
                value = jnp.where((lane + (TURNS - which)) % TURNS == k, turned[k], value)
            out.append(value)
    cell_total = jnp.maximum(sum(flags[1:], flags[0]), 1.0) * cells
    mean = sum(sums[1:], sums[0]) / cell_total
    second = jnp.zeros_like(mean)
    for b in range(samples):
        shift = sums[b] / cells - mean
        second = second + squares[b] + flags[b] * cells * shift * shift
    scale = lax.rsqrt(second / cell_total + field_eps)
    mean, scale = (jnp.concatenate([x] * (patches // LANES), axis=1) for x in (mean, scale))
    normed = ((fields_ref[...].astype(f32) - mean) * scale).astype(bf16)
    tokens = lax.dot_general(
        normed, weight_ref[...], (((0,), (0,)), ((), ())), preferred_element_type=f32
    )
    tokens = tokens + embed_ref[...].astype(f32)
    for j in range(groups):
        rows[pl.ds(j, patches, stride=groups), :] = tokens[:, j * LANES : (j + 1) * LANES]
    tokens_ref[...] = rows[...].reshape(tokens_ref.shape).astype(bf16)
    row = lax.broadcasted_iota(jnp.int32, (normed_ref.shape[0] - pixels, patches), 0)
    padded = jnp.concatenate([normed.astype(f32), jnp.where(row == 0, 1.0, 0.0)], axis=0)
    row = lax.broadcasted_iota(jnp.int32, (patches, patches), 0)
    lane = lax.broadcasted_iota(jnp.int32, (patches, patches), 1)
    half = patches // 2
    source = jnp.where(lane < half, 2 * lane, 2 * (lane - half) + 1)
    order = jnp.where(row == source, 1.0, 0.0).astype(bf16)
    normed_ref[...] = jnp.dot(padded.astype(bf16), order, preferred_element_type=f32).astype(bf16)


def head_lanes(width):
    row = lax.broadcasted_iota(jnp.int32, (LANES, width), 0)
    lane = lax.broadcasted_iota(jnp.int32, (LANES, width), 1)
    head = lane // (width // HEADS)
    return jnp.where((row % HEADS == head) & (row < 3 * HEADS), 1.0, 0.0).astype(bf16)


def head_sums(values, sums_ref, first, slots, head_dim):
    for p in range(sums_ref.shape[0]):
        for i in range(0, values.shape[1], LANES):
            block = jnp.transpose(values[p * slots : (p + 1) * slots, i : i + LANES])
            for k in range(LANES // head_dim):
                head = (first + i) // head_dim + k
                sums_ref[p, head : head + 1, :] = jnp.sum(
                    block[k * head_dim : (k + 1) * head_dim], axis=0, keepdims=True
                )


def three_parts(values):
    high = values.astype(bf16).astype(f32)
    rest = values - high
    middle = rest.astype(bf16).astype(f32)
    empty = jnp.zeros((LANES - 3 * HEADS, values.shape[1]), f32)
    parts = jnp.concatenate([high, middle, rest - middle, empty], axis=0)
    return jnp.transpose(parts).astype(bf16)


def mix_kernel(
    presence_ref,
    slot_ref,
    recv_ref,
    key_ref,
    value_ref,
    query_ref,
    grad_ref,
    mixed_ref,
    send_ref,
    arrived,
    tokens,
    keys,
    values,
    key_grad,
    value_grad,
    leaving,
    squares,
    raw,
    attn_grad,
):
    slots, recv_rows, _ = recv_ref.shape
    width = key_ref.shape[0]
    groups = width // LANES
    send_rows = send_ref.shape[1]
    head_dim = width // HEADS
    score_scale = 1.0 / math.sqrt(head_dim)
    pairs = recv_rows // groups
    spans = [slice(c, c + SPAN) for c in range(0, width, SPAN)]
    halves = [slice(p * slots, (p + 1) * slots) for p in range(pairs)]

    arrived[...] = recv_ref[...].astype(f32).reshape(arrived.shape)
    for p in range(pairs):
        for j in range(groups):
            block = arrived[pl.ds(p * groups + j, slots, stride=recv_rows), :]
            tokens[halves[p], j * LANES : (j + 1) * LANES] = block.astype(bf16)

    row = lax.broadcasted_iota(jnp.int32, (LANES, slots), 0)
    lookup = jnp.where(row == slot_ref[...], 1.0, 0.0).astype(bf16)
    present = jnp.broadcast_to(presence_ref[...].astype(f32), (HEADS, LANES)).astype(bf16)
    valid = jnp.dot(present, lookup, preferred_element_type=f32) > 0.5

    query = query_ref[...]
    grad = grad_ref[...].astype(f32)
    spread = head_lanes(width)
    for span in spans:
        block = jnp.dot(tokens[...], key_ref[:, span], preferred_element_type=f32)
        keys[:, span] = block
        head_sums(block * block, squares, span.start, slots, head_dim)
        head_sums(block * query[:, span], raw, span.start, slots, head_dim)
    for span in spans:
        block = jnp.dot(tokens[...], value_ref[:, span], preferred_element_type=f32)
        values[:, span] = block
        block = jnp.concatenate([block[halves[p]] * grad[p : p + 1, span] for p in range(pairs)], axis=0)
        head_sums(block, attn_grad, span.start, slots, head_dim)

    attention_parts, along_parts, across_parts = [], [], []
    for p in range(pairs):
        ratio = lax.rsqrt(squares[p] * (1.0 / head_dim) + key_eps)
        scores = raw[p] * ratio * score_scale
        top = jnp.max(jnp.where(valid, scores, masked_low), axis=1, keepdims=True)
        weights = jnp.where(valid, jnp.exp(scores - top), 0.0)
        change = attn_grad[p]
        inner = jnp.sum(weights * change, axis=1, keepdims=True)
        share = 1.0 / jnp.sum(weights, axis=1, keepdims=True)
        weights = weights * share
        inner = inner * share
        dscore = weights * (change - inner)
        attention_parts.append(three_parts(weights))
        along_parts.append(three_parts(dscore * ratio * score_scale))
        across_parts.append(three_parts(dscore * scores * ratio * ratio * (1.0 / head_dim)))
    attention_parts = jnp.concatenate(attention_parts, axis=0)
    along_parts = jnp.concatenate(along_parts, axis=0)
    across_parts = jnp.concatenate(across_parts, axis=0)

    for span in spans:
        weights = jnp.dot(attention_parts, spread[:, span], preferred_element_type=f32)
        first = jnp.dot(along_parts, spread[:, span], preferred_element_type=f32)
        second = jnp.dot(across_parts, spread[:, span], preferred_element_type=f32)
        key_block = keys[:, span]
        key_grad[:, span] = (first * query[:, span] - second * key_block).astype(bf16)
        dquery = jnp.sum(first * key_block, axis=0, keepdims=True)
        for p in range(pairs):
            part = weights[halves[p]]
            value_grad[halves[p], span] = (part * grad[p : p + 1, span]).astype(bf16)
            mixed_ref[p : p + 1, span] = jnp.sum(
                part * values[halves[p], span], axis=0, keepdims=True
            ).astype(bf16)
        for i in range(SPAN // LANES):
            j = span.start // LANES + i
            line = dquery[:, i * LANES : (i + 1) * LANES]
            leaving[pl.ds(pairs * groups + j, slots, stride=send_rows), :] = jnp.broadcast_to(
                line, (slots, LANES)
            )

    contract = (((1,), (1,)), ((), ()))
    for span in spans:
        block = lax.dot_general(key_grad[...], key_ref[span, :], contract, preferred_element_type=f32)
        block = block + lax.dot_general(
            value_grad[...], value_ref[span, :], contract, preferred_element_type=f32
        )
        for p in range(pairs):
            for i in range(SPAN // LANES):
                j = span.start // LANES + i
                leaving[pl.ds(p * groups + j, slots, stride=send_rows), :] = block[
                    halves[p], i * LANES : (i + 1) * LANES
                ]
    send_ref[...] = leaving[...].reshape(send_ref.shape).astype(bf16)


def mix_scratch(pairs, slots, width, rows, groups):
    return [
        pltpu.VMEM((slots * rows, LANES), f32),
        pltpu.VMEM((pairs * slots, width), bf16),
        pltpu.VMEM((pairs * slots, width), f32),
        pltpu.VMEM((pairs * slots, width), f32),
        pltpu.VMEM((pairs * slots, width), bf16),
        pltpu.VMEM((pairs * slots, width), bf16),
        pltpu.VMEM((slots * (rows + groups), LANES), f32),
        pltpu.VMEM((pairs, HEADS, slots), f32),
        pltpu.VMEM((pairs, HEADS, slots), f32),
        pltpu.VMEM((pairs, HEADS, slots), f32),
    ]


def grad_kernel(recv_ref, normed_ref, out_ref, arrived, grads, packed):
    owners, recv_rows, _ = recv_ref.shape
    width = grads.shape[1]
    groups = width // LANES
    pairs = recv_rows // groups - 1
    copies, out_rows, _ = out_ref.shape
    pixels = out_rows // groups - 2
    blocks = recv_ref[...].astype(f32)
    arrived[...] = blocks.reshape(arrived.shape)
    dquery = jnp.sum(blocks[:, pairs * groups :, :], axis=0)
    for p in range(pairs):
        for j in range(groups):
            block = arrived[pl.ds(p * groups + j, owners, stride=recv_rows), :]
            grads[p * owners : (p + 1) * owners, j * LANES : (j + 1) * LANES] = block.astype(bf16)
    sums = jnp.dot(normed_ref[...], grads[...], preferred_element_type=f32)
    for j in range(groups):
        lanes = slice(j * LANES, (j + 1) * LANES)
        packed[j * pixels : (j + 1) * pixels, :] = sums[:pixels, lanes]
        packed[groups * pixels + j : groups * pixels + j + 1, :] = sums[pixels : pixels + 1, lanes]
    packed[groups * (pixels + 1) :, :] = dquery
    total = packed[...].astype(bf16)
    for c in range(copies):
        out_ref[c] = total


def total_kernel(parts_ref, weight_ref, embed_ref, query_ref):
    pixels, width = weight_ref.shape
    groups = width // LANES
    parts = [parts_ref[b].astype(f32) for b in range(parts_ref.shape[0])]
    total = sum(parts[1:], parts[0])
    for j in range(groups):
        lanes = slice(j * LANES, (j + 1) * LANES)
        weight_ref[:, lanes] = total[j * pixels : (j + 1) * pixels]
        embed_ref[:, lanes] = total[groups * pixels + j : groups * pixels + j + 1]
        query_ref[:, lanes] = total[groups * (pixels + 1) + j : groups * (pixels + 1) + j + 1]


vmem = pl.BlockSpec(memory_space=pltpu.VMEM)
hbm = pl.BlockSpec(memory_space=pltpu.HBM)


def on_device(
    fields, presence, slot_var, patch_weight, var_embed, query, key_weight, value_weight, out_grad
):
    var_count = lax.axis_size("var")
    _, _, patches, pixels = fields.shape
    width = key_weight.shape[0]
    groups = width // LANES
    slots = slot_var.shape[0]
    pairs = patches // var_count
    rows = pairs * groups
    samples = lax.axis_size("dp")
    fixed = tuple(
        pltpu.with_memory_space_constraint(a, pltpu.HBM)
        for a in (
            jnp.transpose(fields.reshape(patches, pixels)),
        patch_weight.reshape(pixels, width),
        var_embed,
        presence,
        slot_var.reshape(1, slots),
        query.reshape(1, width),
        out_grad.reshape(pairs, width),
        )
    )

    stats, fields, patch_weight, var_embed, present, slot_row, query_row, grad_rows = pl.pallas_call(
        stats_kernel,
        out_shape=(pltpu.VMEM((1, LANES), f32),)
        + tuple(pltpu.VMEM(a.shape, a.dtype) for a in fixed),
        in_specs=[hbm] * len(fixed),
        out_specs=[vmem] * (1 + len(fixed)),
        scratch_shapes=[pltpu.SemaphoreType.DMA((len(fixed),))],
        name="stats",
    )(*fixed)
    stats = lax.all_gather(stats, "dp")

    tokens, normed = pl.pallas_call(
        token_kernel,
        out_shape=(
            jax.ShapeDtypeStruct((var_count, rows, LANES), bf16),
            jax.ShapeDtypeStruct((2 * pixels, patches), bf16),
        ),
        in_specs=[vmem] * 4,
        out_specs=(vmem, vmem),
        scratch_shapes=[pltpu.VMEM((patches * groups, LANES), f32)],
        compiler_params=params(16),
        cost_estimate=pl.CostEstimate(flops=6 * 10**9, bytes_accessed=2 * 10**6, transcendentals=0),
        name="tokens",
    )(stats, fields, patch_weight, var_embed)
    gathered = lax.all_to_all(tokens, "var", split_axis=0, concat_axis=0, tiled=True)

    mixed, outgoing = pl.pallas_call(
        mix_kernel,
        out_shape=(
            jax.ShapeDtypeStruct((pairs, width), bf16),
            jax.ShapeDtypeStruct((slots, rows + groups, LANES), bf16),
        ),
        in_specs=[vmem] * 7,
        out_specs=(vmem, vmem),
        scratch_shapes=mix_scratch(pairs, slots, width, rows, groups),
        compiler_params=params(32),
        name="mix",
    )(present, slot_row, gathered, key_weight, value_weight, query_row, grad_rows)
    returned = lax.all_to_all(outgoing, "var", split_axis=0, concat_axis=0, tiled=True)

    parts = pl.pallas_call(
        grad_kernel,
        out_shape=jax.ShapeDtypeStruct((samples, groups * (pixels + 2), LANES), bf16),
        in_specs=[vmem, vmem],
        out_specs=vmem,
        scratch_shapes=[
            pltpu.VMEM((var_count * (rows + groups), LANES), f32),
            pltpu.VMEM((patches, width), bf16),
            pltpu.VMEM((groups * (pixels + 2), LANES), f32),
        ],
        compiler_params=params(16),
        name="grads",
    )(returned, normed)
    parts = lax.all_to_all(parts, "dp", split_axis=0, concat_axis=0, tiled=True)

    dweight, dembed, dquery = pl.pallas_call(
        total_kernel,
        out_shape=(
            jax.ShapeDtypeStruct((pixels, width), f32),
            jax.ShapeDtypeStruct((1, width), f32),
            jax.ShapeDtypeStruct((1, width), f32),
        ),
        in_specs=[vmem],
        out_specs=(vmem, vmem, vmem),
        compiler_params=params(16),
        name="totals",
    )(parts)
    return (
        mixed.reshape(1, pairs, width),
        dweight.reshape(1, pixels, width),
        dembed,
        dquery.reshape(width),
    )


def solution(mesh):
    return jax.shard_map(
        on_device,
        mesh=mesh,
        in_specs=(
            P("dp", "var", None, None),
            P("dp", None),
            P(),
            P("var", None, None),
            P("var", None),
            P(),
            P(),
            P(),
            P("dp", "var", None),
        ),
        out_specs=(P("dp", "var", None), P("var", None, None), P("var", None), P()),
        check_vma=False,
    )
```
